512 devices in a mesh: dp: 16 (over z), tensor: 32 (over x, y, core).
Axes of the slice: x: 4, y: 4, z: 16, core: 2. Of those that a mesh axis runs over, the one named last changes fastest.
Arguments:
- context: bfloat16 [3072, 16384], P('tensor', 'dp'), may hold values from -6 to 6
- residual: bfloat16 [6144, 16384], P('tensor', 'dp'), may hold values from -110 to 110
- out_weight: bfloat16 [6144, 3072], P('tensor', 'dp'), may hold values from -0.109375 to 0.109375
- norm_gain: float32 [6144], P('tensor'), may hold values from 0.25 to 1.75
- norm_bias: float32 [6144], P('tensor'), may hold values from -4 to 4
- target: bfloat16 [6144, 16384], P('tensor', 'dp'), may hold values from -5 to 5
- probe: bfloat16 [6144, 3072], P('tensor'), may hold values from -1 to 1, as said below
Outputs:
- hess_diag: float32 [6144, 3072], P('tensor', 'dp')
- residual_grad: float32 [6144, 16384], P('tensor', 'dp')
The draws below stay inside these ranges and needn't reach their ends.
Inputs may be any that keep to these rules, and one draw needn't show every extreme that they name: `probe`: every entry is -1 or +1.
All inputs are finite; a program needn't handle non-finite values.
Results may differ from the reference program's by a relative error of at most 0.0014.
Values may be sent and summed in bfloat16 or wider, within the bound.
A program may use at most 64 MiB of HBM per device.

```python
import math
import jax
import jax.numpy as jnp
from jax import lax

D = 6144
K = 3072
TOK_DEV = 1024
TOKENS = 16384
N_DP = 16


def draw_residual(key, part):
    key = jax.random.fold_in(key, 2)
    key_base, key_rows, key_cols = jax.random.split(key, 3)
    position = (jnp.arange(D, dtype=jnp.float32) / (D - 1) - 0.5)[:, None]
    col_scale = jnp.exp(jax.random.uniform(key_cols, (D, 1), jnp.float32, math.log(0.3), math.log(3.0)))
    base_draw = jnp.clip(jax.random.normal(key_base, (D, TOKENS), jnp.float32), -5.0, 5.0)
    col_ramp = jnp.exp(position * math.log(3.0))
    row_scale = jnp.exp(jax.random.uniform(key_rows, (1, TOKENS), jnp.float32, math.log(0.4), math.log(4.0)))
    return (base_draw * row_scale * col_scale * col_ramp).astype(jnp.bfloat16)


def draw_probe(key, part):
    key = jax.random.fold_in(key, 7)
    coin_bits = jax.random.randint(key, (D, K), 0, 2)
    return (2.0 * coin_bits.astype(jnp.float32) - 1.0).astype(jnp.bfloat16)


def strengthened(values, stream_key, source, target, blocks, factor):
    def block_of(axis_at):
        return (jnp.arange(values.shape[axis_at]) // (values.shape[axis_at] // blocks)).reshape((-1,) + (1,) * (values.ndim - 1 - axis_at))

    near = jax.random.permutation(stream_key, blocks)[block_of(target)]
    other_side = (block_of(target) + blocks // 2) % blocks
    return jnp.where((block_of(source) == near) | (block_of(source) == other_side), factor * values, values)


def steps_of(key, dims, pieces, low, top_value):
    gain = 1.0
    for dim, parts in pieces:
        heights = jax.random.uniform(jax.random.fold_in(jax.random.fold_in(key, 6), dim), (parts,), jnp.float32, low / len(pieces), top_value / len(pieces))
        gain = gain * jnp.repeat(jnp.exp(heights), dims[dim] // parts).reshape((-1,) + (1,) * (len(dims) - 1 - dim))
    return gain


def gaussian(rng, dims, width, reach, pieces=(), held_as=jnp.bfloat16):
    array = width * jax.random.normal(rng, dims, jnp.float32)
    if pieces:
        array = array * steps_of(rng, dims, pieces, -0.22, 0.18)
    return jnp.clip(array, -reach, reach).astype(held_as)


def noise_with(key, extent, spread, limit, pieces, heavy, kind=jnp.bfloat16):
    result = spread * jax.random.normal(key, extent, jnp.float32)
    if pieces:
        result = result * steps_of(key, extent, pieces, -0.22, 0.18)
    return jnp.clip(strengthened(result, jax.random.fold_in(key, 3), *heavy), -limit, limit).astype(kind)


def setup_inputs(seed: int = 0) -> dict:
    key_of = jax.random.split(jax.random.key(seed), 8)
    context = noise_with(key_of[0], (K, TOKENS), 1.0, 6.0, ((0, 32), (1, 16)), (1, 0, 32, 2.75))
    residual = draw_residual(jax.random.fold_in(key_of[7], 71), 0)
    out_weight = gaussian(key_of[2], (D, K), K ** -0.5, 0.109375, ((0, 32), (1, 16)))
    norm_gain = jnp.clip(1.0 + 0.15 * jax.random.normal(key_of[3], (D,), jnp.float32), 0.25, 1.75)
    norm_bias = gaussian(key_of[4], (D,), 1.0, 4.0, ((0, 32),), jnp.float32)
    target = gaussian(key_of[5], (D, TOKENS), 1.0, 5.0, ((0, 32), (1, 16)))
    probe = draw_probe(jax.random.fold_in(key_of[7], 71), 0)
    return dict(context=context, residual=residual, out_weight=out_weight, norm_gain=norm_gain, norm_bias=norm_bias, target=target, probe=probe)


def token_block(weight, probe, norm_gain, norm_bias, block):
    ctx, res, tgt = block
    proj = jnp.dot(ctx, weight, preferred_element_type=jnp.float32)
    tangent = jnp.dot(ctx, probe, preferred_element_type=jnp.float32)
    resid = res.astype(jnp.float32) + proj
    row_mean = lax.optimization_barrier(jnp.sum(resid, axis=1, keepdims=True)) / D
    cent = resid - row_mean
    inv_scale = 1.0 / jnp.sqrt(lax.optimization_barrier(jnp.sum(cent * cent, axis=1, keepdims=True)) / D + 1e-05)
    normed = cent * inv_scale
    grad_normed = norm_gain * (norm_gain * normed + norm_bias - tgt.astype(jnp.float32))
    grad_mean = lax.optimization_barrier(jnp.sum(grad_normed, axis=1, keepdims=True)) / D
    grad_proj = lax.optimization_barrier(jnp.sum(grad_normed * normed, axis=1, keepdims=True)) / D
    residual_grad = inv_scale * (grad_normed - grad_mean - normed * grad_proj)
    tan_mean = lax.optimization_barrier(jnp.sum(tangent, axis=1, keepdims=True)) / D
    tan_proj = lax.optimization_barrier(jnp.sum(normed * tangent, axis=1, keepdims=True)) / D
    tan_normed = inv_scale * (tangent - tan_mean - normed * tan_proj)
    tan_grad = norm_gain * norm_gain * tan_normed
    curv_mean = lax.optimization_barrier(jnp.sum(tan_grad, axis=1, keepdims=True)) / D
    curv_proj = lax.optimization_barrier(jnp.sum(tan_grad * normed + grad_normed * tan_normed, axis=1, keepdims=True)) / D
    curvature = -inv_scale * tan_proj * residual_grad + inv_scale * (tan_grad - curv_mean - tan_normed * grad_proj - normed * curv_proj)
    curvature = curvature.astype(jnp.bfloat16)
    partial_value = jnp.dot(ctx.T, curvature, preferred_element_type=jnp.float32)
    return (partial_value, residual_grad)

def reference(context, residual, out_weight, norm_gain, norm_bias, target, probe):
    weight = out_weight.T
    probe_kd = probe.T
    blocks = (context.T.reshape(N_DP, TOK_DEV, K), residual.T.reshape(N_DP, TOK_DEV, D), target.T.reshape(N_DP, TOK_DEV, D))

    def step_fn(running, block):
        partial_value, residual_grad = token_block(weight, probe_kd, norm_gain, norm_bias, block)
        return (running + partial_value, residual_grad)
    start_sum = jnp.zeros((K, D), jnp.float32)
    summed, grads = lax.scan(step_fn, start_sum, blocks)
    hess_diag = probe_kd.astype(jnp.float32) * summed / (TOK_DEV * N_DP)
    return (hess_diag.T, grads.reshape(TOK_DEV * N_DP, D).T)
```

```python
import jax
import jax.numpy as jnp
from jax import lax
from jax.experimental import pallas as pl
from jax.experimental.pallas import tpu as pltpu
from jax.sharding import PartitionSpec as P

MESH = pl.DeviceIdType.MESH
F32 = jnp.float32
BF16 = jnp.bfloat16

D = 6144
ROWS = 192
TOK = 1024
BLK = 96
NZ = 16
NT = 32
PK = 288
SUB = 144
TOKENS = 16384


def kernel(
    ctx_in, res_in, w_in, gain_ref, bias_ref, tgt_in, probe_in,
    hess_ref, rg_out,
    ctx, stk, pk, wloc, probe, res, tgt, xv, tau, gainb, biasb, mom, mbuf, cbuf, curv, curvt, rg, rs,
    load_sem, ctx_send, p_recv, q_recv, c_recv, pk_send, pkr_recv, pkl_recv,
    mom_send, mom_recv, cf_send, cf_recv, rs_send, rsr_recv, rsl_recv,
):
    z = lax.axis_index("dp")
    t = lax.axis_index("tensor")
    core = lax.rem(t, 2)
    x = lax.div(t, 8)
    y = lax.rem(lax.div(t, 2), 4)
    p = x + core * (y - x)
    q = y + core * (x - y)
    sp = 8 - 6 * core
    sq = 2 + 6 * core

    def dev(dp, dq):
        return lax.rem(p + dp + 4, 4) * sp + lax.rem(q + dq + 4, 4) * sq + core

    other = t + 1 - 2 * core
    z_up = lax.rem(z + 1, NZ)
    z_down = lax.rem(z + NZ - 1, NZ)

    def wait_bytes(ref, sem):
        pltpu.make_async_copy(ref, ref, sem).wait()

    def send(src, dst, ssem, rsem, zz, tt):
        pltpu.make_async_remote_copy(
            src_ref=src, dst_ref=dst, send_sem=ssem, recv_sem=rsem, device_id=(zz, tt), device_id_type=MESH
        ).start()

    own_rows = pl.ds(pl.multiple_of(t * BLK, 32), BLK)
    loads = [
        pltpu.make_async_copy(w_in, wloc, load_sem.at[0]),
        pltpu.make_async_copy(probe_in, probe, load_sem.at[1]),
        pltpu.make_async_copy(ctx_in, ctx.at[own_rows, :], load_sem.at[2]),
        pltpu.make_async_copy(res_in, res, load_sem.at[3]),
        pltpu.make_async_copy(tgt_in, tgt, load_sem.at[4]),
    ]
    for c in loads:
        c.start()

    barrier = pltpu.get_barrier_semaphore()
    for zz in (z_up, z_down):
        pl.semaphore_signal(barrier, inc=1, device_id=(zz, t), device_id_type=MESH)

    def greet(i, carry):
        pl.semaphore_signal(barrier, inc=1, device_id=(z, lax.rem(t + i, NT)), device_id_type=MESH)
        return carry

    lax.fori_loop(1, NT, greet, 0)
    pl.semaphore_wait(barrier, NT + 1)

    def rows_of(dp, dq):
        return pl.ds(pl.multiple_of(dev(dp, dq) * BLK, 32), BLK)

    def blk(dp, dq, half=None):
        if half is None:
            return ctx.at[rows_of(dp, dq), :]
        return ctx.at[rows_of(dp, dq), pl.ds(half * 512, 512)]

    def to_core(dp, dq, src=None):
        b = blk(dp, dq)
        send(b if src is None else src, b, ctx_send, c_recv.at[(dp % 4) * 4 + dq % 4], z, other)

    def along_q(dp, src=None):
        b = blk(dp, 0)
        s = b if src is None else src
        send(s, b, ctx_send, q_recv.at[(dp % 4) * 4 + 0], z, dev(0, 1))
        send(s, b, ctx_send, q_recv.at[(dp % 4) * 4 + 1], z, dev(0, -1))

    own = ctx.at[own_rows, :]
    send(ctx_in, own, ctx_send, p_recv.at[0], z, dev(1, 0))
    send(ctx_in, own, ctx_send, p_recv.at[1], z, dev(-1, 0))
    along_q(0, ctx_in)
    to_core(0, 0, ctx_in)

    def pk_sub(j, s):
        return pk.at[j, pl.ds(s * SUB, SUB), :]

    def pk_send_to(j, s, up, step):
        ref = pk_sub(j, s)
        if up:
            send(ref, ref, pk_send, pkr_recv.at[step * 2 + s], z_up, t)
        else:
            send(ref, ref, pk_send, pkl_recv.at[step * 2 + s], z_down, t)

    loads[0].wait()
    pk[z, 0:192, :] = wloc[:, 0:128]
    pk[z, 192:288, 0:64] = wloc[0:96, 128:192]
    pk[z, 192:288, 64:128] = wloc[96:192, 128:192]
    for s in range(2):
        pk_send_to(z, s, True, 0)
        pk_send_to(z, s, False, 0)

    def unpack(j):
        stk[j, 0:192, 0:128] = pk[j, 0:192, :]
        stk[j, 0:96, 128:192] = pk[j, 192:288, 0:64]
        stk[j, 96:192, 128:192] = pk[j, 192:288, 64:128]

    def z_step(n):
        below = lax.rem(z + NZ - n, NZ)
        above = lax.rem(z + n, NZ)
        for s in range(2):
            if n < 8 or s == 0:
                wait_bytes(pk_sub(below, s), pkr_recv.at[(n - 1) * 2 + s])
                if n < 7 or (n == 7 and s == 0):
                    pk_send_to(below, s, True, n)
            if n < 8 or s == 1:
                wait_bytes(pk_sub(above, s), pkl_recv.at[(n - 1) * 2 + s])
                if n < 7 or (n == 7 and s == 1):
                    pk_send_to(above, s, False, n)
        unpack(below)
        if n < 8:
            unpack(above)

    unpack(z)
    loads[1].wait()
    for j in range(NZ):
        stk[j, 192:384, :] = probe[:, 192 * j : 192 * (j + 1)]
    gainb[...] = jnp.transpose(jnp.broadcast_to(gain_ref[...], (128, ROWS)))
    biasb[...] = jnp.transpose(jnp.broadcast_to(bias_ref[...], (128, ROWS)))

    def take_p(dp):
        wait_bytes(blk(dp, 0), p_recv.at[0 if dp < 0 else 1])
        half = 0 if dp < 0 else 1
        b = blk(dp, 0, half)
        send(b, b, ctx_send, p_recv.at[2 + half], z, dev(-dp, 0))
        along_q(dp)
        to_core(dp, 0)

    def take_p2():
        for half in range(2):
            wait_bytes(blk(2, 0, half), p_recv.at[2 + half])
        along_q(2)
        to_core(2, 0)

    def take_q(dp):
        for dq in (-1, 1):
            half = 0 if dq < 0 else 1
            wait_bytes(blk(dp, dq), q_recv.at[(dp % 4) * 4 + half])
            b = blk(dp, dq, half)
            send(b, b, ctx_send, q_recv.at[(dp % 4) * 4 + 2 + half], z, dev(0, -dq))
            to_core(dp, dq)

    def take_q2(dp):
        for half in range(2):
            wait_bytes(blk(dp, 2, half), q_recv.at[(dp % 4) * 4 + 2 + half])
        to_core(dp, 2)

    take_p(-1)
    take_p(1)
    z_step(1)
    take_q(0)
    take_p2()
    z_step(2)
    take_q(-1)
    z_step(3)
    take_q(1)
    z_step(4)
    take_q2(0)
    take_q(2)
    z_step(5)
    take_q2(-1)
    z_step(6)
    take_q2(1)
    z_step(7)
    take_q2(2)
    z_step(8)
    for c in loads[2:]:
        c.wait()

    def other_rows(dp, dq):
        osp = 2 + 6 * core
        osq = 8 - 6 * core
        o = lax.rem(q + dp + 4, 4) * osp + lax.rem(p + dq + 4, 4) * osq + 1 - core
        return ctx.at[pl.ds(pl.multiple_of(o * BLK, 32), BLK), :]

    for dp in range(4):
        for dq in range(4):
            wait_bytes(other_rows(dp, dq), c_recv.at[dp * 4 + dq])

    for n in range(4):
        cols = slice(n * 256, (n + 1) * 256)

        def add(j, carry):
            rows = pl.ds(pl.multiple_of(j * 192, 64), 192)
            return carry + jnp.dot(stk[j], ctx[rows, cols], preferred_element_type=F32)

        both = lax.fori_loop(0, NZ, add, jnp.zeros((384, 256), F32))
        xv[:, cols] = both[0:192]
        tau[:, cols] = both[192:384]

    def sums(k, carry):
        lanes = pl.ds(pl.multiple_of(k * 128, 128), 128)
        tot = jnp.zeros((16, 128), F32)
        for r in range(12):
            rows = pl.ds(r * 16, 16)
            xx = xv[rows, lanes] + res[rows, lanes].astype(F32)
            xv[rows, lanes] = xx
            tot = tot + xx
        mean = jnp.sum(tot, axis=0, keepdims=True) / ROWS
        accs = [jnp.zeros((16, 128), F32) for _ in range(11)]
        for r in range(12):
            rows = pl.ds(r * 16, 16)
            yy = xv[rows, lanes] - mean
            tt = tau[rows, lanes]
            g = gainb[rows, :]
            w = g * g
            h = g * (biasb[rows, :] - tgt[rows, lanes].astype(F32))
            wy = w * yy
            wt = w * tt
            terms = (yy * yy, wy, wy * yy, h, h * yy, tt, yy * tt, wt, wy * tt, h * tt, w)
            accs = [a + b for a, b in zip(accs, terms)]
        mom[k, 0:1, :] = mean
        for i in range(11):
            mom[k, i + 1 : i + 2, :] = jnp.sum(accs[i], axis=0, keepdims=True)
        return carry

    mom[...] = jnp.zeros((8, 16, 128), F32)
    lax.fori_loop(0, 8, sums, 0)

    mine = lax.div(t, 4)
    is_owner = lax.rem(t, 4) == 0
    for k in range(8):

        @pl.when(t != 4 * k)
        def _():
            send(mom.at[k], mbuf.at[t], mom_send, mom_recv, z, 4 * k)

    @pl.when(is_owner)
    def _():
        mbuf[t] = mom[mine]
        wait_bytes(mbuf.at[pl.ds(0, NT - 1)], mom_recv)
        (mi, yy, wy, wyy, h, hy, tt, yt, wt, wyt, ht, w) = [mbuf[:, i, :] for i in range(12)]

        def total(a):
            return jnp.sum(a, axis=0, keepdims=True)

        mean = total(mi) / NT
        d = mi - mean
        s_zz = total(yy + ROWS * d * d)
        s_wz = total(wy + d * w)
        s_wzz = total(wyy + d * (2 * wy + d * w))
        s_h = total(h)
        s_hz = total(hy + d * h)
        s_t = total(tt)
        s_zt = total(yt + d * tt)
        s_wt = total(wt)
        s_wzt = total(wyt + d * wt)
        s_ht = total(ht)
        s_w = total(w)
        sc = 1.0 / jnp.sqrt(s_zz / D + 1e-05)
        s_wn = sc * s_wz
        s_wnn = sc * sc * s_wzz
        s_hn = sc * s_hz
        g_mean = (s_wn + s_h) / D
        g_proj = (s_wnn + s_hn) / D
        t_mean = s_t / D
        t_proj = sc * s_zt / D
        c_mean = sc * (s_wt - t_mean * s_w - t_proj * s_wn) / D
        c_proj = sc * (2 * (sc * s_wzt - t_mean * s_wn - t_proj * s_wnn) + s_ht - t_mean * s_h - t_proj * s_hn) / D
        for i, v in enumerate((mean, sc, g_mean, g_proj, t_mean, t_proj, c_mean, c_proj)):
            cbuf[mine, i : i + 1, :] = v

        def tell(i, carry):
            send(cbuf.at[mine], cbuf.at[mine], cf_send, cf_recv.at[mine], z, lax.rem(t + i, NT))
            return carry

        lax.fori_loop(1, NT, tell, 0)

    for k in range(8):

        @pl.when(t != 4 * k)
        def _():
            wait_bytes(cbuf.at[k], cf_recv.at[k])

    def finish(k, carry):
        lanes = pl.ds(pl.multiple_of(k * 128, 128), 128)
        mean, sc, g_mean, g_proj, t_mean, t_proj, c_mean, c_proj = [cbuf[k, i : i + 1, :] for i in range(8)]
        lead = -sc * t_proj
        for r in range(12):
            rows = pl.ds(r * 16, 16)
            n = (xv[rows, lanes] - mean) * sc
            g = gainb[rows, :]
            w = g * g
            gn = g * (g * n + biasb[rows, :] - tgt[rows, lanes].astype(F32))
            grad = sc * (gn - g_mean - n * g_proj)
            rg[rows, lanes] = grad
            u = sc * (tau[rows, lanes] - t_mean - n * t_proj)
            cv = lead * grad + sc * (w * u - c_mean - u * g_proj - n * c_proj)
            curv[rows, :] = cv
            if r >= 8:
                curv[pl.ds(r * 16 + 64, 16), :] = cv
        curvt[pl.ds(pl.multiple_of(k * 128, 128), 128), :] = jnp.transpose(curv[...]).astype(BF16)
        return carry

    lax.fori_loop(0, 8, finish, 0)
    rg_copy = pltpu.make_async_copy(rg, rg_out, load_sem.at[5])
    rg_copy.start()

    rsr = rs.at[pl.ds(0, 9)]
    rsl = rs.at[pl.ds(9, 9)]

    def product(j):
        rows = pl.ds(pl.multiple_of(j * 192, 64), 192)
        full = jnp.dot(ctx[rows, :], curvt[...], preferred_element_type=F32)
        lane = lax.broadcasted_iota(jnp.int32, (96, 128), 1)
        return full[:, 0:128], jnp.where(lane < 64, full[0:96, 128:256], full[96:192, 128:256])

    def put(buf, n, j, add):
        a, b = product(j)
        if add:
            buf[n, 0:192, :] = buf[n, 0:192, :] + a
            buf[n, 192:288, :] = buf[n, 192:288, :] + b
        else:
            buf[n, 0:192, :] = a
            buf[n, 192:288, :] = b

    def rs_send_to(buf, n, s, up):
        src = buf.at[n, pl.ds(s * SUB, SUB), :]
        dst = buf.at[n + 1, pl.ds(s * SUB, SUB), :]
        if up:
            send(src, dst, rs_send, rsr_recv.at[n * 2 + s], z_up, t)
        else:
            send(src, dst, rs_send, rsl_recv.at[n * 2 + s], z_down, t)

    far = lax.rem(z + 8, NZ)
    put(rsr, 0, far, False)
    rs_send_to(rsr, 0, 0, True)
    src = rsr.at[0, pl.ds(SUB, SUB), :]
    send(src, rsl.at[1, pl.ds(SUB, SUB), :], rs_send, rsl_recv.at[1], z_down, t)
    for n in range(1, 8):
        for up in (True, False):
            buf, sem = (rsr, rsr_recv) if up else (rsl, rsl_recv)
            j = lax.rem(z + 8 - n, NZ) if up else lax.rem(z + 8 + n, NZ)
            a, b = product(j)
            if n == 1:
                s = 0 if up else 1
                wait_bytes(buf.at[n, pl.ds(s * SUB, SUB), :], sem.at[(n - 1) * 2 + s])
                lo = 0 if up else SUB
                whole = jnp.concatenate([a, b], axis=0)
                buf[n, lo : lo + SUB, :] = buf[n, lo : lo + SUB, :] + whole[lo : lo + SUB]
                rs_send_to(buf, n, s, up)
                buf[n, SUB - lo : 2 * SUB - lo, :] = whole[SUB - lo : 2 * SUB - lo]
                rs_send_to(buf, n, 1 - s, up)
            else:
                whole = jnp.concatenate([a, b], axis=0)
                for s in range(2):
                    lo = s * SUB
                    wait_bytes(buf.at[n, pl.ds(lo, SUB), :], sem.at[(n - 1) * 2 + s])
                    buf[n, lo : lo + SUB, :] = buf[n, lo : lo + SUB, :] + whole[lo : lo + SUB]
                    rs_send_to(buf, n, s, up)
    a, b = product(z)
    for s in range(2):
        wait_bytes(rsr.at[8, pl.ds(s * SUB, SUB), :], rsr_recv.at[14 + s])
        wait_bytes(rsl.at[8, pl.ds(s * SUB, SUB), :], rsl_recv.at[14 + s])
    a = a + rsr[8, 0:192, :] + rsl[8, 0:192, :]
    b = b + rsr[8, 192:288, :] + rsl[8, 192:288, :]
    at = jnp.transpose(a)
    bt = jnp.transpose(b)
    pc = stk[z, 192:384, :].astype(F32)
    hess_ref[0:128, :] = pc[0:128] * at / TOKENS
    hess_ref[128:192, 0:96] = pc[128:192, 0:96] * bt[0:64] / TOKENS
    hess_ref[128:192, 96:192] = pc[128:192, 96:192] * bt[64:128] / TOKENS

    rg_copy.wait()
    wait_bytes(ctx.at[pl.ds(0, 31 * BLK), :], ctx_send)
    wait_bytes(pk.at[pl.ds(0, 15)], pk_send)
    wait_bytes(rs.at[pl.ds(0, 15)], rs_send)

    @pl.when(is_owner)
    def _():
        wait_bytes(mom.at[pl.ds(0, 7)], mom_send)
        wait_bytes(rs.at[0, pl.ds(0, 8 * (NT - 1)), :], cf_send)

    @pl.when(jnp.logical_not(is_owner))
    def _():
        wait_bytes(mom, mom_send)


def shards(context, residual, out_weight, norm_gain, norm_bias, target, probe):
    hbm = pl.BlockSpec(memory_space=pl.ANY)
    vmem = pl.BlockSpec(memory_space=pltpu.VMEM)
    dma = pltpu.SemaphoreType.DMA
    return pl.pallas_call(
        kernel,
        out_shape=(
            jax.ShapeDtypeStruct((ROWS, 192), F32),
            jax.ShapeDtypeStruct((ROWS, TOK), F32),
        ),
        in_specs=[hbm, hbm, hbm, vmem, vmem, hbm, hbm],
        out_specs=(vmem, hbm),
        scratch_shapes=[
            pltpu.VMEM((NT * BLK, TOK), BF16),
            pltpu.VMEM((NZ, 384, 192), BF16),
            pltpu.VMEM((NZ, PK, 128), BF16),
            pltpu.VMEM((192, 192), BF16),
            pltpu.VMEM((ROWS, 3072), BF16),
            pltpu.VMEM((ROWS, TOK), BF16),
            pltpu.VMEM((ROWS, TOK), BF16),
            pltpu.VMEM((ROWS, TOK), F32),
            pltpu.VMEM((ROWS, TOK), F32),
            pltpu.VMEM((ROWS, 128), F32),
            pltpu.VMEM((ROWS, 128), F32),
            pltpu.VMEM((8, 16, 128), F32),
            pltpu.VMEM((NT, 16, 128), F32),
            pltpu.VMEM((8, 8, 128), F32),
            pltpu.VMEM((256, 128), F32),
            pltpu.VMEM((TOK, 256), BF16),
            pltpu.VMEM((ROWS, TOK), F32),
            pltpu.VMEM((18, PK, 128), F32),
            dma((6,)),
            dma,
            dma((4,)),
            dma((16,)),
            dma((16,)),
            dma,
            dma((16,)),
            dma((16,)),
            dma,
            dma,
            dma,
            dma((8,)),
            dma,
            dma((16,)),
            dma((16,)),
        ],
        compiler_params=pltpu.CompilerParams(
            collective_id=0, has_side_effects=True, vmem_limit_bytes=48 * 1024 * 1024
        ),
    )(context, residual, out_weight, norm_gain.reshape(1, ROWS), norm_bias.reshape(1, ROWS), target, probe)


def solution(mesh):
    return jax.shard_map(
        shards,
        mesh=mesh,
        in_specs=(
            P("tensor", "dp"),
            P("tensor", "dp"),
            P("tensor", "dp"),
            P("tensor"),
            P("tensor"),
            P("tensor", "dp"),
            P("tensor", None),
        ),
        out_specs=(P("tensor", "dp"), P("tensor", "dp")),
        check_vma=False,
    )
```

```python
import jax
import jax.numpy as jnp
from jax import lax
from jax.experimental import pallas as pl
from jax.experimental.pallas import tpu as pltpu
from jax.sharding import PartitionSpec as P

MESH = pl.DeviceIdType.MESH
F32 = jnp.float32
BF16 = jnp.bfloat16

D = 6144
ROWS = 192
TOK = 1024
BLK = 96
NZ = 16
NT = 32
PK = 288
SUB = 144
TOKENS = 16384

PLAN = (
    ("S", "p", 1), ("S", "p", -1), ("S", "zu", 1, 0), ("S", "zd", 1, 1), ("S", "zd", 1, 0), ("S", "zu", 1, 1),
    ("W", "zu", 1, 0), ("S", "zu", 2, 0), ("S", "q", 0, -1), ("S", "q", 0, 1), ("W", "zd", 1, 1), ("S", "zd", 2, 1),
    ("W", "zd", 1, 0), ("W", "zu", 1, 1), ("W", "p", 1), ("S", "zu", 2, 1), ("W", "p", -1), ("S", "p2", 1),
    ("S", "zd", 2, 0), ("W", "zu", 2, 0), ("S", "zu", 3, 0), ("S", "q", -1, -1), ("W", "zd", 2, 1), ("S", "zd", 3, 1),
    ("W", "zu", 2, 1), ("W", "zd", 2, 0), ("S", "zu", 3, 1), ("S", "q", 1, 1), ("S", "zd", 3, 0), ("S", "p2", 0),
    ("W", "zu", 3, 0), ("S", "zu", 4, 0), ("W", "zd", 3, 1), ("S", "zd", 4, 1), ("W", "zu", 3, 1), ("S", "zu", 4, 1),
    ("S", "q", 1, -1), ("W", "p2", 1), ("W", "zd", 3, 0), ("S", "q", -1, 1), ("S", "zd", 4, 0), ("W", "zu", 4, 0),
    ("S", "zu", 5, 0), ("W", "zd", 4, 1), ("S", "zd", 5, 1), ("W", "q", 1, 1), ("W", "p2", 0), ("W", "q", -1, -1),
    ("S", "q2h", 0, 1), ("W", "zu", 4, 1), ("S", "q2h", 1, 1), ("S", "zu", 5, 1), ("S", "q2h", 0, -1),
    ("S", "qq", -1, 0), ("W", "q", 0, 1), ("W", "zd", 4, 0), ("S", "zd", 5, 0), ("W", "zu", 5, 0), ("S", "zu", 6, 0),
    ("S", "q2h", 1, -1), ("W", "zd", 5, 1), ("S", "zd", 6, 1), ("W", "zu", 5, 1), ("S", "qq", 1, 1),
    ("S", "qq", 0, 1), ("S", "zu", 6, 1), ("W", "zd", 5, 0), ("W", "q", 0, -1), ("S", "zd", 6, 0), ("S", "qq", 0, 0),
    ("W", "zu", 6, 0), ("S", "zu", 7, 0), ("W", "q", 1, -1), ("W", "zd", 6, 1), ("S", "zd", 7, 1), ("W", "q", -1, 1),
    ("S", "qq", 1, 0), ("S", "qq", -1, 1), ("W", "zd", 6, 0), ("W", "q2h", 1, 1), ("W", "zu", 6, 1),
    ("W", "q2h", 0, -1), ("S", "zd", 7, 0), ("S", "zu", 7, 1), ("S", "qq", 2, 0), ("S", "qq", 2, 1),
    ("W", "zu", 7, 0), ("S", "zu", 8, 0), ("W", "zd", 7, 1), ("S", "zd", 8, 1), ("W", "qq", 1, 1),
    ("W", "q2h", 1, -1), ("W", "qq", -1, 1), ("W", "qq", -1, 0), ("W", "qq", 0, 1), ("W", "zu", 7, 1),
    ("W", "zd", 7, 0), ("W", "qq", 0, 0), ("W", "q2h", 0, 1), ("W", "qq", 1, 0), ("W", "zu", 8, 0), ("W", "qq", 2, 0),
    ("W", "qq", 2, 1), ("W", "zd", 8, 1),
)

def kernel(
    ctx_in, res_in, w_in, gain_in, bias_in, tgt_in, probe_in,
    hess_ref, rg_out,
    ctx, stk, pk, wloc, res, tgt, xv, tau, grow, brow, gainb, biasb, mom, mbuf, cbuf, curv, curvt, rg, rs, prod,
    load_sem, ctx_send, p_recv, q_recv, c_recv, pk_send, pkr_recv, pkl_recv,
    mom_send, mom_recv, cf_send, cf_recv, rs_send, rsr_recv, rsl_recv,
):
    z = lax.axis_index("dp")
    t = lax.axis_index("tensor")
    core = lax.rem(t, 2)
    x = lax.div(t, 8)
    y = lax.rem(lax.div(t, 2), 4)
    p = x + core * (y - x)
    q = y + core * (x - y)
    sp = 8 - 6 * core
    sq = 2 + 6 * core

    def dev(dp, dq):
        return lax.rem(p + dp + 4, 4) * sp + lax.rem(q + dq + 4, 4) * sq + core

    other = t + 1 - 2 * core
    z_up = lax.rem(z + 1, NZ)
    z_down = lax.rem(z + NZ - 1, NZ)

    def wait_bytes(ref, sem):
        pltpu.make_async_copy(ref, ref, sem).wait()

    def send(src, dst, ssem, rsem, zz, tt):
        pltpu.make_async_remote_copy(
            src_ref=src, dst_ref=dst, send_sem=ssem, recv_sem=rsem, device_id=(zz, tt), device_id_type=MESH
        ).start()

    barrier = pltpu.get_barrier_semaphore()
    for zz in (z_up, z_down):
        pl.semaphore_signal(barrier, inc=1, device_id=(zz, t), device_id_type=MESH)

    def greet(i, carry):
        pl.semaphore_signal(barrier, inc=1, device_id=(z, lax.rem(t + i, NT)), device_id_type=MESH)
        return carry

    lax.fori_loop(1, NT, greet, 0)

    own_rows = pl.ds(pl.multiple_of(t * BLK, 32), BLK)
    own = ctx.at[own_rows, :]
    loads = [
        pltpu.make_async_copy(w_in, wloc, load_sem.at[0]),
        pltpu.make_async_copy(probe_in, stk.at[pl.ds(ROWS, ROWS), :], load_sem.at[1]),
        pltpu.make_async_copy(ctx_in, own, load_sem.at[2]),
        pltpu.make_async_copy(res_in, res, load_sem.at[3]),
        pltpu.make_async_copy(tgt_in, tgt, load_sem.at[4]),
        pltpu.make_async_copy(gain_in, grow, load_sem.at[6]),
        pltpu.make_async_copy(bias_in, brow, load_sem.at[7]),
    ]
    for c in loads:
        c.start()
    loads[0].wait()
    pk[z, 0:192, :] = wloc[:, 0:128]
    pk[z, 192:288, 0:64] = wloc[0:96, 128:192]
    pk[z, 192:288, 64:128] = wloc[96:192, 128:192]
    pl.semaphore_wait(barrier, NT + 1)

    def blk(dp, dq, half=None):
        rows = pl.ds(pl.multiple_of(dev(dp, dq) * BLK, 32), BLK)
        if half is None:
            return ctx.at[rows, :]
        return ctx.at[rows, pl.ds(half * 512, 512)]

    def to_core(dp, dq, src=None):
        b = blk(dp, dq)
        send(b if src is None else src, b, ctx_send, c_recv.at[(dp % 4) * 4 + dq % 4], z, other)

    def route(kind, a, b=None):
        if kind == "p":
            return blk(a, 0), p_recv.at[0 if a < 0 else 1], (0, 0, None), (-a, 0)
        if kind == "p2":
            d = -1 if a == 0 else 1
            return blk(2, 0, a), p_recv.at[2 + a], (d, 0, a), (-d, 0)
        if kind == "q":
            return blk(a, b), q_recv.at[(a % 4) * 6 + (0 if b < 0 else 1)], (a, 0, None), (0, -b)
        if kind == "q2h":
            return blk(2, b, a), q_recv.at[12 + (0 if b < 0 else 1) + 2 * a], (2, 0, a), (0, -b)
        d = -1 if b == 0 else 1
        return blk(a, 2, b), q_recv.at[(a % 4) * 6 + 4 + b], (a, d, b), (0, -d)

    def pk_sub(j, s):
        return pk.at[j, pl.ds(s * SUB, SUB), :]

    def z_block(up, n):
        return lax.rem(z + NZ - n, NZ) if up else lax.rem(z + n, NZ)

    arrived = set()
    for act, kind, *ab in PLAN:
        if kind in ("zu", "zd"):
            n, s = ab
            up = kind == "zu"
            sem = (pkr_recv if up else pkl_recv).at[(n - 1) * 2 + s]
            if act == "S":
                ref = pk_sub(z_block(up, n - 1), s)
                send(ref, ref, pk_send, sem, z_up if up else z_down, t)
            else:
                wait_bytes(pk_sub(z_block(up, n), s), sem)
            continue
        dst, sem, (dp, dq, half), to = route(kind, *ab)
        if act == "S":
            src = blk(dp, dq, half)
            if (dp, dq) == (0, 0):
                send(ctx_in, src, ctx_send, sem, z, dev(*to))
                if kind == "q" and ab[1] == 1:
                    to_core(0, 0, ctx_in)
            else:
                send(src, src, ctx_send, sem, z, dev(*to))
            continue
        wait_bytes(dst, sem)
        arrived.add((kind, *ab))
        if kind == "p":
            to_core(ab[0], 0)
        elif kind == "q":
            to_core(*ab)
        elif kind == "p2" and ("p2", 1 - ab[0]) in arrived:
            to_core(2, 0)
        elif kind == "q2h" and ("q2h", 1 - ab[0], ab[1]) in arrived:
            to_core(2, ab[1])
        elif kind == "qq" and ("qq", ab[0], 1 - ab[1]) in arrived:
            to_core(ab[0], 2)

    for c in loads[5:]:
        c.wait()
    gainb[...] = jnp.transpose(jnp.broadcast_to(grow[...], (128, ROWS)))
    biasb[...] = jnp.transpose(jnp.broadcast_to(brow[...], (128, ROWS)))
    for j in range(NZ):
        c = 192 * j
        stk[0:192, c : c + 128] = pk[j, 0:192, :]
        stk[0:96, c + 128 : c + 192] = pk[j, 192:288, 0:64]
        stk[96:192, c + 128 : c + 192] = pk[j, 192:288, 64:128]

    for c in loads[1:5]:
        c.wait()

    def other_rows(dp, dq):
        osp = 2 + 6 * core
        osq = 8 - 6 * core
        o = lax.rem(q + dp + 4, 4) * osp + lax.rem(p + dq + 4, 4) * osq + 1 - core
        return ctx.at[pl.ds(pl.multiple_of(o * BLK, 32), BLK), :]

    for dp in range(4):
        for dq in range(4):
            wait_bytes(other_rows(dp, dq), c_recv.at[dp * 4 + dq])

    for n in range(2):
        cols = slice(n * 512, (n + 1) * 512)
        both = jnp.dot(stk[...], ctx[:, cols], preferred_element_type=F32)
        xv[:, cols] = both[0:192]
        tau[:, cols] = both[192:384]

    def sums(k, carry):
        lanes = pl.ds(pl.multiple_of(k * 128, 128), 128)
        tot = jnp.zeros((16, 128), F32)
        for r in range(12):
            rows = pl.ds(r * 16, 16)
            xx = xv[rows, lanes] + res[rows, lanes].astype(F32)
            xv[rows, lanes] = xx
            tot = tot + xx
        mean = jnp.sum(tot, axis=0, keepdims=True) / ROWS
        accs = [jnp.zeros((16, 128), F32) for _ in range(11)]
        for r in range(12):
            rows = pl.ds(r * 16, 16)
            yy = xv[rows, lanes] - mean
            tt = tau[rows, lanes]
            g = gainb[rows, :]
            w = g * g
            h = g * (biasb[rows, :] - tgt[rows, lanes].astype(F32))
            wy = w * yy
            wt = w * tt
            terms = (yy * yy, wy, wy * yy, h, h * yy, tt, yy * tt, wt, wy * tt, h * tt, w)
            accs = [a + b for a, b in zip(accs, terms)]
        mom[k, 0:1, :] = mean
        for i in range(11):
            mom[k, i + 1 : i + 2, :] = jnp.sum(accs[i], axis=0, keepdims=True)
        mom[k, 12:16, :] = jnp.ones((4, 128), F32)

        @pl.when(t != 4 * k + 1)
        def _():
            send(mom.at[k], mbuf.at[t], mom_send, mom_recv, z, 4 * k + 1)

        return carry

    lax.fori_loop(0, 8, sums, 0)
    mine = lax.div(t, 4)
    is_owner = lax.rem(t, 4) == 1

    @pl.when(is_owner)
    def _():
        mbuf[t] = mom[mine]
        wait_bytes(mbuf.at[pl.ds(0, NT - 1)], mom_recv)
        s0 = mbuf[0]
        for i in range(1, NT):
            s0 = s0 + mbuf[i]
        mean = s0[0:1] / NT
        s1 = jnp.zeros((16, 128), F32)
        s2 = jnp.zeros((16, 128), F32)
        for i in range(NT):
            m = mbuf[i]
            dm = (m[0:1] - mean) * m
            s1 = s1 + dm
            s2 = s2 + (m[0:1] - mean) * dm

        def row(a, i):
            return a[i : i + 1]

        s_w = row(s0, 11)
        s_h = row(s0, 4)
        s_t = row(s0, 6)
        s_wt = row(s0, 8)
        s_ht = row(s0, 10)
        s_zz = row(s0, 1) + ROWS * row(s2, 12)
        s_wz = row(s0, 2) + row(s1, 11)
        s_wzz = row(s0, 3) + 2 * row(s1, 2) + row(s2, 11)
        s_hz = row(s0, 5) + row(s1, 4)
        s_zt = row(s0, 7) + row(s1, 6)
        s_wzt = row(s0, 9) + row(s1, 8)
        sc = 1.0 / jnp.sqrt(s_zz / D + 1e-05)
        s_wn = sc * s_wz
        s_wnn = sc * sc * s_wzz
        s_hn = sc * s_hz
        g_mean = (s_wn + s_h) / D
        g_proj = (s_wnn + s_hn) / D
        t_mean = s_t / D
        t_proj = sc * s_zt / D
        c_mean = sc * (s_wt - t_mean * s_w - t_proj * s_wn) / D
        c_proj = sc * (2 * (sc * s_wzt - t_mean * s_wn - t_proj * s_wnn) + s_ht - t_mean * s_h - t_proj * s_hn) / D
        for i, v in enumerate((mean, sc, g_mean, g_proj, t_mean, t_proj, c_mean, c_proj)):
            cbuf[mine, i : i + 1, :] = v

        def tell(i, carry):
            send(cbuf.at[mine], cbuf.at[mine], cf_send, cf_recv.at[mine], z, lax.rem(t + i, NT))
            return carry

        lax.fori_loop(1, NT, tell, 0)

    for k in range(8):

        @pl.when(t != 4 * k + 1)
        def _():
            wait_bytes(cbuf.at[k], cf_recv.at[k])

    def finish(k, carry):
        lanes = pl.ds(pl.multiple_of(k * 128, 128), 128)
        mean, sc, g_mean, g_proj, t_mean, t_proj, c_mean, c_proj = [cbuf[k, i : i + 1, :] for i in range(8)]
        lead = -sc * t_proj
        for r in range(12):
            rows = pl.ds(r * 16, 16)
            n = (xv[rows, lanes] - mean) * sc
            g = gainb[rows, :]
            w = g * g
            gn = g * (g * n + biasb[rows, :] - tgt[rows, lanes].astype(F32))
            grad = sc * (gn - g_mean - n * g_proj)
            rg[rows, lanes] = grad
            u = sc * (tau[rows, lanes] - t_mean - n * t_proj)
            cv = lead * grad + sc * (w * u - c_mean - u * g_proj - n * c_proj)
            curv[rows, :] = cv
            if r >= 8:
                curv[pl.ds(r * 16 + 64, 16), :] = cv
        curvt[pl.ds(pl.multiple_of(k * 128, 128), 128), :] = jnp.transpose(curv[...]).astype(BF16)
        return carry

    lax.fori_loop(0, 8, finish, 0)
    rg_copy = pltpu.make_async_copy(rg, rg_out, load_sem.at[5])
    rg_copy.start()

    def product(j, slot):
        rows = pl.ds(pl.multiple_of(j * 192, 64), 192)
        full = jnp.dot(ctx[rows, :], curvt[...], preferred_element_type=F32)
        lane = lax.broadcasted_iota(jnp.int32, (96, 128), 1)
        prod[slot, 0:192, :] = full[:, 0:128]
        prod[slot, 192:288, :] = jnp.where(lane < 64, full[0:96, 128:256], full[96:192, 128:256])

    def rs_sub(w, n, s):
        return rs.at[w * 9 + n, pl.ds(s * SUB, SUB), :]

    def rs_take(w, n, s):
        wait_bytes(rs_sub(w, n, s), (rsr_recv if w == 0 else rsl_recv).at[(n - 1) * 2 + s])

    def rs_pass(w, n, s):
        sem = (rsr_recv if w == 0 else rsl_recv).at[n * 2 + s]
        send(rs_sub(w, n, s), rs_sub(w, n + 1, s), rs_send, sem, z_up if w == 0 else z_down, t)

    def span(s):
        return slice(s * SUB, (s + 1) * SUB)

    product(lax.rem(z + 8, NZ), 0)
    for w in range(2):
        rs[w * 9, span(w), :] = prod[0, span(w), :]
        rs_pass(w, 0, w)
    for n in range(1, 8):
        product(lax.rem(z + 8 - n, NZ), 0)
        product(lax.rem(z + 8 + n, NZ), 1)
        for first in (True, False):
            for w in range(2):
                s = 1 - w if first else w
                if n == 1 and first:
                    rs[w * 9 + n, span(s), :] = prod[w, span(s), :]
                else:
                    rs_take(w, n, s)
                    rs[w * 9 + n, span(s), :] = rs[w * 9 + n, span(s), :] + prod[w, span(s), :]
                rs_pass(w, n, s)
    product(z, 0)
    pair = stk[192:384, pl.ds(pl.multiple_of(lax.div(z, 2) * 384, 128), 384)].astype(F32)
    pc = jnp.where(lax.rem(z, 2) == 0, pair[:, 0:192], pair[:, 192:384]) * (1.0 / TOKENS)
    for w in range(2):
        for s in range(2):
            rs_take(w, 8, s)
    both = prod[0] + rs[8] + rs[17]
    at = jnp.transpose(both[0:192])
    bt = jnp.transpose(both[192:288])
    hess_ref[0:128, :] = pc[0:128] * at
    hess_ref[128:192, 0:96] = pc[128:192, 0:96] * bt[0:64]
    hess_ref[128:192, 96:192] = pc[128:192, 96:192] * bt[64:128]

    rg_copy.wait()
    wait_bytes(ctx.at[pl.ds(0, 31 * BLK), :], ctx_send)
    wait_bytes(pk.at[pl.ds(0, 15)], pk_send)
    wait_bytes(rs.at[pl.ds(0, 15)], rs_send)

    @pl.when(is_owner)
    def _():
        wait_bytes(mom.at[pl.ds(0, 7)], mom_send)
        wait_bytes(rs.at[0, pl.ds(0, 8 * (NT - 1)), :], cf_send)

    @pl.when(jnp.logical_not(is_owner))
    def _():
        wait_bytes(mom, mom_send)


def shards(context, residual, out_weight, norm_gain, norm_bias, target, probe):
    hbm = pl.BlockSpec(memory_space=pltpu.HBM)
    anywhere = pl.BlockSpec(memory_space=pl.ANY)
    vmem = pl.BlockSpec(memory_space=pltpu.VMEM)
    dma = pltpu.SemaphoreType.DMA
    arrays = (context, residual, out_weight, norm_gain.reshape(1, ROWS), norm_bias.reshape(1, ROWS), target, probe)
    arrays = [pltpu.with_memory_space_constraint(a, pltpu.HBM) for a in arrays]
    return pl.pallas_call(
        kernel,
        out_shape=(
            jax.ShapeDtypeStruct((ROWS, 192), F32),
            jax.ShapeDtypeStruct((ROWS, TOK), F32),
        ),
        in_specs=[hbm] * 7,
        out_specs=(vmem, anywhere),
        scratch_shapes=[
            pltpu.VMEM((NT * BLK, TOK), BF16),
            pltpu.VMEM((2 * ROWS, 3072), BF16),
            pltpu.VMEM((NZ, PK, 128), BF16),
            pltpu.VMEM((192, 192), BF16),
            pltpu.VMEM((ROWS, TOK), BF16),
            pltpu.VMEM((ROWS, TOK), BF16),
            pltpu.VMEM((ROWS, TOK), F32),
            pltpu.VMEM((ROWS, TOK), F32),
            pltpu.VMEM((1, ROWS), F32),
            pltpu.VMEM((1, ROWS), F32),
            pltpu.VMEM((ROWS, 128), F32),
            pltpu.VMEM((ROWS, 128), F32),
            pltpu.VMEM((8, 16, 128), F32),
            pltpu.VMEM((NT, 16, 128), F32),
            pltpu.VMEM((8, 8, 128), F32),
            pltpu.VMEM((256, 128), F32),
            pltpu.VMEM((TOK, 256), BF16),
            pltpu.VMEM((ROWS, TOK), F32),
            pltpu.VMEM((18, PK, 128), F32),
            pltpu.VMEM((2, PK, 128), F32),
            dma((8,)),
            dma,
            dma((4,)),
            dma((24,)),
            dma((16,)),
            dma,
            dma((16,)),
            dma((16,)),
            dma,
            dma,
            dma,
            dma((8,)),
            dma,
            dma((16,)),
            dma((16,)),
        ],
        compiler_params=pltpu.CompilerParams(
            collective_id=0, has_side_effects=True, vmem_limit_bytes=48 * 1024 * 1024
        ),
    )(*arrays)


def solution(mesh):
    return jax.shard_map(
        shards,
        mesh=mesh,
        in_specs=(
            P("tensor", "dp"),
            P("tensor", "dp"),
            P("tensor", "dp"),
            P("tensor"),
            P("tensor"),
            P("tensor", "dp"),
            P("tensor", None),
        ),
        out_specs=(P("tensor", "dp"), P("tensor", "dp")),
        check_vma=False,
    )
```

```python
import jax
import jax.numpy as jnp
from jax import lax
from jax.experimental import pallas as pl
from jax.experimental.pallas import tpu as pltpu
from jax.sharding import PartitionSpec as P

MESH = pl.DeviceIdType.MESH
F32 = jnp.float32
BF16 = jnp.bfloat16

D = 6144
ROWS = 192
TOK = 1024
BLK = 96
NZ = 16
NT = 32
PK = 288
ZSUB = 192
RSUB = 144
RMSG = 224
LOW = 2.0**-8 / 10
FAST = 2 * 3
TOKENS = 16384

PLAN = (
    (
        ("S", "p", 1), ("S", "p", -1), ("S", "q", 0, 1), ("S", "q", 0, -1), ("W", "p", 1), ("S", "q", 1, 1),
        ("W", "p", -1), ("S", "q", -1, -1), ("W", "q", 0, 1), ("S", "p2", 0), ("S", "p2", 1), ("S", "qq", 0, 1),
        ("W", "p2", 0), ("S", "q2h", 0, -1), ("S", "q", -1, 1), ("W", "p2", 1), ("W", "q", -1, -1),
        ("S", "q2h", 1, 1), ("S", "q", 1, -1), ("W", "q", 0, -1), ("W", "q", 1, 1), ("S", "qq", -1, 0),
        ("S", "q2h", 0, 1), ("S", "qq", 1, 1), ("S", "qq", 0, 0), ("W", "q2h", 0, -1), ("S", "q2h", 1, -1),
        ("W", "q2h", 1, 1), ("S", "qq", 2, 1), ("S", "qq", 2, 0), ("W", "q", -1, 1), ("W", "q", 1, -1),
        ("S", "qq", 1, 0), ("S", "qq", -1, 1), ("W", "q2h", 0, 1), ("W", "qq", 2, 1), ("W", "qq", -1, 0),
        ("W", "qq", 2, 0), ("W", "q2h", 1, -1), ("W", "qq", -1, 1), ("W", "qq", 0, 1), ("W", "qq", 1, 1),
        ("W", "qq", 0, 0), ("W", "qq", 1, 0),
    ),
    (
        ("S", "p", -1), ("S", "zd", 2, 0), ("S", "zu", 2, 0), ("S", "p", 1), ("S", "q", 0, -1), ("S", "zu", 2, 1),
        ("S", "zd", 1, 0), ("S", "zu", 2, 2), ("S", "zd", 2, 2), ("S", "zd", 2, 1), ("W", "p", -1), ("S", "zd", 1, 2),
        ("S", "zu", 1, 0), ("W", "p", 1), ("S", "q", 1, 1), ("S", "q", -1, -1), ("S", "q", 1, -1), ("S", "q", -1, 1),
        ("S", "p2", 1), ("S", "zd", 1, 1), ("S", "zu", 1, 1), ("W", "zu", 2, 0), ("S", "zu", 4, 0), ("S", "p2", 0),
        ("W", "zd", 2, 0), ("S", "zd", 4, 0), ("W", "zu", 2, 2), ("W", "zu", 2, 1), ("W", "zd", 2, 2),
        ("S", "zu", 3, 1), ("W", "zd", 2, 1), ("S", "zu", 1, 2), ("S", "zd", 4, 2), ("W", "q", 0, -1),
        ("S", "zu", 4, 1), ("S", "zd", 3, 0), ("W", "zd", 1, 1), ("W", "p2", 0), ("S", "zd", 4, 1), ("S", "zu", 4, 2),
        ("S", "q", 0, 1), ("W", "zu", 4, 0), ("S", "zd", 3, 2), ("S", "q2h", 0, -1), ("W", "zd", 4, 0),
        ("S", "zu", 6, 0), ("S", "zd", 5, 0), ("W", "zd", 4, 2), ("S", "zd", 6, 2), ("S", "zu", 5, 0),
        ("W", "zu", 4, 1), ("S", "zu", 6, 1), ("W", "zd", 3, 0), ("W", "q", -1, -1), ("W", "zu", 1, 1),
        ("W", "q", -1, 1), ("S", "qq", -1, 1), ("W", "p2", 1), ("W", "zd", 1, 0), ("W", "q", 1, -1),
        ("S", "q2h", 1, 1), ("W", "zu", 1, 0), ("W", "q", 1, 1), ("S", "qq", 0, 0), ("S", "zd", 6, 0),
        ("W", "zu", 1, 2), ("W", "zu", 4, 2), ("S", "zu", 6, 2), ("W", "zd", 4, 1), ("S", "zd", 6, 1),
        ("W", "zu", 6, 0), ("S", "zu", 3, 0), ("W", "q2h", 0, -1), ("S", "qq", -1, 0), ("W", "zd", 3, 2),
        ("S", "qq", 2, 0), ("S", "q2h", 0, 1), ("S", "qq", 1, 0), ("W", "zd", 5, 0), ("S", "zd", 5, 2),
        ("W", "zu", 5, 0), ("S", "zu", 5, 1), ("S", "zu", 7, 0), ("W", "zd", 6, 2), ("S", "zd", 7, 2),
        ("W", "zu", 3, 1), ("S", "qq", 1, 1), ("W", "q", 0, 1), ("S", "qq", 0, 1), ("W", "zu", 6, 1),
        ("S", "zu", 7, 1), ("S", "zd", 5, 1), ("W", "q2h", 1, 1), ("S", "zu", 5, 2), ("S", "zd", 3, 1),
        ("S", "qq", 2, 1), ("W", "zu", 6, 2), ("S", "zu", 3, 2), ("W", "zd", 6, 0), ("S", "zu", 7, 2),
        ("S", "zd", 7, 0), ("W", "zd", 6, 1), ("S", "zd", 7, 1), ("S", "q2h", 1, -1), ("W", "zu", 5, 1),
        ("W", "zu", 7, 0), ("S", "zu", 8, 0), ("W", "zd", 7, 2), ("S", "zd", 8, 2), ("W", "zu", 3, 0),
        ("W", "zu", 7, 1), ("S", "zu", 8, 1), ("W", "qq", 0, 0), ("W", "zu", 5, 2), ("W", "qq", 2, 0),
        ("W", "zu", 7, 2), ("W", "qq", 1, 0), ("W", "zd", 5, 2), ("W", "zd", 3, 1), ("W", "qq", -1, 0),
        ("W", "zd", 7, 1), ("W", "q2h", 0, 1), ("W", "zd", 5, 1), ("W", "zu", 3, 2), ("W", "qq", 2, 1),
        ("W", "q2h", 1, -1), ("W", "zd", 1, 2), ("W", "zu", 8, 0), ("W", "qq", 0, 1), ("W", "zd", 7, 0),
        ("W", "qq", -1, 1), ("W", "qq", 1, 1), ("W", "zd", 8, 2), ("W", "zu", 8, 1),
    ),
)

def kernel(
    ctx_in, res_in, w_in, gain_in, bias_in, tgt_in, probe_in,
    hess_ref, rg_out,
    ctx, stk, pk, wloc, res, tgt, xv, tau, grow, brow, gainb, biasb, mom, mbuf, cbuf, curv, curvt, rg, rs, prod, prod0, back,
    load_sem, ctx_send, p_recv, q_recv, c_recv, pk_send, pkr_recv, pkl_recv, w_send, w_recv,
    mom_send, mom_recv, cf_send, cf_recv, rs_send, rsr_recv, rsl_recv, prod_send, prod_recv, back_send, back_recv,
):
    z = lax.axis_index("dp")
    t = lax.axis_index("tensor")
    core = lax.rem(t, 2)
    x = lax.div(t, 8)
    y = lax.rem(lax.div(t, 2), 4)
    other = t + 1 - 2 * core
    is_one = core == 1
    is_zero = core == 0

    def plane(n):
        return lax.rem(z + n + NZ, NZ)


    def wait_bytes(ref, sem):
        pltpu.make_async_copy(ref, ref, sem).wait()

    def send(src, dst, ssem, rsem, zz, tt):
        pltpu.make_async_remote_copy(
            src_ref=src, dst_ref=dst, send_sem=ssem, recv_sem=rsem, device_id=(zz, tt), device_id_type=MESH
        ).start()

    barrier = pltpu.get_barrier_semaphore()
    for n in (1, -1, 2, -2):
        pl.semaphore_signal(barrier, inc=1, device_id=(plane(n), t), device_id_type=MESH)

    def greet(i, carry):
        pl.semaphore_signal(barrier, inc=1, device_id=(z, lax.rem(t + i, NT)), device_id_type=MESH)
        return carry

    lax.fori_loop(1, NT, greet, 0)

    own_rows = pl.ds(pl.multiple_of(t * BLK, 32), BLK)
    own = ctx.at[own_rows, :]
    loads = [
        pltpu.make_async_copy(w_in, wloc, load_sem.at[0]),
        pltpu.make_async_copy(probe_in, stk.at[pl.ds(ROWS, ROWS), :], load_sem.at[1]),
        pltpu.make_async_copy(ctx_in, own, load_sem.at[2]),
        pltpu.make_async_copy(res_in, res, load_sem.at[3]),
        pltpu.make_async_copy(tgt_in, tgt, load_sem.at[4]),
        pltpu.make_async_copy(gain_in, grow, load_sem.at[6]),
        pltpu.make_async_copy(bias_in, brow, load_sem.at[7]),
    ]
    for c in loads:
        c.start()
    loads[0].wait()
    half_at = pl.multiple_of((1 - core) * PK, 32)
    pk[z, pl.ds(half_at, 192), :] = wloc[:, 0:128]
    pk[z, pl.ds(half_at + 192, 96), 0:64] = wloc[0:96, 128:192]
    pk[z, pl.ds(half_at + 192, 96), 64:128] = wloc[96:192, 128:192]
    pl.semaphore_wait(barrier, NT + 3)

    def zero_half(j):
        return pk.at[j, pl.ds(PK, PK), :]

    def pk_sub(j, s):
        return pk.at[j, pl.ds(s * ZSUB, ZSUB), :]

    def gather(c):
        p, q = (y, x) if c else (x, y)
        sp, sq = (2, 8) if c else (8, 2)

        def dev(dp, dq):
            return lax.rem(p + dp + 4, 4) * sp + lax.rem(q + dq + 4, 4) * sq + c

        def blk(dp, dq, half=None):
            rows = pl.ds(pl.multiple_of(dev(dp, dq) * BLK, 32), BLK)
            if half is None:
                return ctx.at[rows, :]
            return ctx.at[rows, pl.ds(half * 512, 512)]

        def to_core(dp, dq, src=None):
            b = blk(dp, dq)
            send(b if src is None else src, b, ctx_send, c_recv.at[(dp % 4) * 4 + dq % 4], z, other)

        def route(kind, a, b=None):
            if kind == "p":
                return blk(a, 0), p_recv.at[0 if a < 0 else 1], (0, 0, None), (-a, 0)
            if kind == "p2":
                d = -1 if a == 0 else 1
                return blk(2, 0, a), p_recv.at[2 + a], (d, 0, a), (-d, 0)
            if kind == "q":
                return blk(a, b), q_recv.at[(a % 4) * 6 + (0 if b < 0 else 1)], (a, 0, None), (0, -b)
            if kind == "q2h":
                return blk(2, b, a), q_recv.at[12 + (0 if b < 0 else 1) + 2 * a], (2, 0, a), (0, -b)
            d = -1 if b == 0 else 1
            return blk(a, 2, b), q_recv.at[(a % 4) * 6 + 4 + b], (a, d, b), (0, -d)

        if c == 0:
            send(zero_half(z), zero_half(z), w_send, w_recv.at[0], z, other)
        arrived = set()
        for act, kind, *ab in PLAN[c]:
            if kind in ("zu", "zd"):
                n, s = ab
                sign = 1 if kind == "zu" else -1
                sem = (pkr_recv if kind == "zu" else pkl_recv).at[(n - 1) * 3 + s]
                hop = 2 if n <= FAST and n % 2 == 0 else 1
                if act == "S":
                    if n == hop and "w" not in arrived:
                        arrived.add("w")
                        wait_bytes(zero_half(z), w_recv.at[0])
                    ref = pk_sub(plane(sign * (hop - n)), s)
                    send(ref, ref, pk_send, sem, plane(sign * hop), t)
                else:
                    j = plane(-sign * n)
                    wait_bytes(pk_sub(j, s), sem)
                    key = n if n == 8 else (kind, n)
                    arrived.add((key, s))
                    if s > 0 and (key, 3 - s) in arrived:
                        send(zero_half(j), zero_half(j), w_send, w_recv.at[n if kind == "zu" or n == 8 else 16 - n], z, other)
                continue
            dst, sem, (dp, dq, half), to = route(kind, *ab)
            if act == "S":
                src = blk(dp, dq, half)
                if (dp, dq) == (0, 0):
                    send(ctx_in, src, ctx_send, sem, z, dev(*to))
                    if kind == "q" and ab[1] == 1:
                        to_core(0, 0, ctx_in)
                else:
                    send(src, src, ctx_send, sem, z, dev(*to))
                continue
            wait_bytes(dst, sem)
            arrived.add((kind, *ab))
            if kind == "p":
                to_core(ab[0], 0)
            elif kind == "q":
                to_core(*ab)
            elif kind == "p2" and ("p2", 1 - ab[0]) in arrived:
                to_core(2, 0)
            elif kind == "q2h" and ("q2h", 1 - ab[0], ab[1]) in arrived:
                to_core(2, ab[1])
            elif kind == "qq" and ("qq", ab[0], 1 - ab[1]) in arrived:
                to_core(ab[0], 2)
        if c == 0:
            for n in range(1, NZ):
                wait_bytes(zero_half(plane(-n)), w_recv.at[n])
        for dp in range(4):
            for dq in range(4):
                o = lax.rem(q + dp + 4, 4) * sq + lax.rem(p + dq + 4, 4) * sp + 1 - c
                rows = pl.ds(pl.multiple_of(o * BLK, 32), BLK)
                wait_bytes(ctx.at[rows, :], c_recv.at[dp * 4 + dq])

    @pl.when(is_zero)
    def _():
        gather(0)

    @pl.when(is_one)
    def _():
        gather(1)

    for c in loads[5:]:
        c.wait()
    gainb[...] = jnp.transpose(jnp.broadcast_to(grow[...], (128, ROWS)))
    biasb[...] = jnp.transpose(jnp.broadcast_to(brow[...], (128, ROWS)))
    for j in range(NZ):
        c = 192 * j
        stk[0:192, c : c + 128] = pk[j, pl.ds(half_at, 192), :]
        stk[0:96, c + 128 : c + 192] = pk[j, pl.ds(half_at + 192, 96), 0:64]
        stk[96:192, c + 128 : c + 192] = pk[j, pl.ds(half_at + 192, 96), 64:128]

    for c in loads[1:5]:
        c.wait()

    for n in range(2):
        cols = slice(n * 512, (n + 1) * 512)
        both = jnp.dot(stk[...], ctx[:, cols], preferred_element_type=F32)
        xv[:, cols] = both[0:192]
        tau[:, cols] = both[192:384]

    def sums(k, carry):
        lanes = pl.ds(pl.multiple_of(k * 128, 128), 128)
        tot = jnp.zeros((16, 128), F32)
        for r in range(12):
            rows = pl.ds(r * 16, 16)
            xx = xv[rows, lanes] + res[rows, lanes].astype(F32)
            xv[rows, lanes] = xx
            tot = tot + xx
        mean = jnp.sum(tot, axis=0, keepdims=True) / ROWS
        accs = [jnp.zeros((16, 128), F32) for _ in range(11)]
        for r in range(12):
            rows = pl.ds(r * 16, 16)
            yy = xv[rows, lanes] - mean
            tt = tau[rows, lanes]
            g = gainb[rows, :]
            w = g * g
            h = g * (biasb[rows, :] - tgt[rows, lanes].astype(F32))
            wy = w * yy
            wt = w * tt
            terms = (yy * yy, wy, wy * yy, h, h * yy, tt, yy * tt, wt, wy * tt, h * tt, w)
            accs = [a + b for a, b in zip(accs, terms)]
        mom[k, 0:1, :] = mean
        for i in range(11):
            mom[k, i + 1 : i + 2, :] = jnp.sum(accs[i], axis=0, keepdims=True)
        mom[k, 12:16, :] = jnp.ones((4, 128), F32)

        @pl.when(t != 4 * k + 1)
        def _():
            send(mom.at[k], mbuf.at[t], mom_send, mom_recv, z, 4 * k + 1)

        return carry

    lax.fori_loop(0, 8, sums, 0)
    mine = lax.div(t, 4)
    is_owner = lax.rem(t, 4) == 1

    @pl.when(is_owner)
    def _():
        mbuf[t] = mom[mine]
        wait_bytes(mbuf.at[pl.ds(0, NT - 1)], mom_recv)
        s0 = mbuf[0]
        for i in range(1, NT):
            s0 = s0 + mbuf[i]
        mean = s0[0:1] / NT
        s1 = jnp.zeros((16, 128), F32)
        s2 = jnp.zeros((16, 128), F32)
        for i in range(NT):
            m = mbuf[i]
            dm = (m[0:1] - mean) * m
            s1 = s1 + dm
            s2 = s2 + (m[0:1] - mean) * dm

        def row(a, i):
            return a[i : i + 1]

        s_w = row(s0, 11)
        s_h = row(s0, 4)
        s_t = row(s0, 6)
        s_wt = row(s0, 8)
        s_ht = row(s0, 10)
        s_zz = row(s0, 1) + ROWS * row(s2, 12)
        s_wz = row(s0, 2) + row(s1, 11)
        s_wzz = row(s0, 3) + 2 * row(s1, 2) + row(s2, 11)
        s_hz = row(s0, 5) + row(s1, 4)
        s_zt = row(s0, 7) + row(s1, 6)
        s_wzt = row(s0, 9) + row(s1, 8)
        sc = 1.0 / jnp.sqrt(s_zz / D + 1e-05)
        s_wn = sc * s_wz
        s_wnn = sc * sc * s_wzz
        s_hn = sc * s_hz
        g_mean = (s_wn + s_h) / D
        g_proj = (s_wnn + s_hn) / D
        t_mean = s_t / D
        t_proj = sc * s_zt / D
        c_mean = sc * (s_wt - t_mean * s_w - t_proj * s_wn) / D
        c_proj = sc * (2 * (sc * s_wzt - t_mean * s_wn - t_proj * s_wnn) + s_ht - t_mean * s_h - t_proj * s_hn) / D
        for i, v in enumerate((mean, sc, g_mean, g_proj, t_mean, t_proj, c_mean, c_proj)):
            cbuf[mine, i : i + 1, :] = v

        def tell(i, carry):
            send(cbuf.at[mine], cbuf.at[mine], cf_send, cf_recv.at[mine], z, lax.rem(t + i, NT))
            return carry

        lax.fori_loop(1, NT, tell, 0)

    for k in range(8):

        @pl.when(t != 4 * k + 1)
        def _():
            wait_bytes(cbuf.at[k], cf_recv.at[k])

    def finish(k, carry):
        lanes = pl.ds(pl.multiple_of(k * 128, 128), 128)
        mean, sc, g_mean, g_proj, t_mean, t_proj, c_mean, c_proj = [cbuf[k, i : i + 1, :] for i in range(8)]
        lead = -sc * t_proj
        for r in range(12):
            rows = pl.ds(r * 16, 16)
            n = (xv[rows, lanes] - mean) * sc
            g = gainb[rows, :]
            w = g * g
            gn = g * (g * n + biasb[rows, :] - tgt[rows, lanes].astype(F32))
            grad = sc * (gn - g_mean - n * g_proj)
            rg[rows, lanes] = grad
            u = sc * (tau[rows, lanes] - t_mean - n * t_proj)
            cv = lead * grad + sc * (w * u - c_mean - u * g_proj - n * c_proj)
            curv[rows, :] = cv
            if r >= 8:
                curv[pl.ds(r * 16 + 64, 16), :] = cv
        curvt[pl.ds(pl.multiple_of(k * 128, 128), 128), :] = jnp.transpose(curv[...]).astype(BF16)
        return carry

    lax.fori_loop(0, 8, finish, 0)
    rg_copy = pltpu.make_async_copy(rg, rg_out, load_sem.at[5])
    rg_copy.start()

    def product(j, slot):
        rows = pl.ds(pl.multiple_of(j * 192, 64), 192)
        full = jnp.dot(ctx[rows, :], curvt[...], preferred_element_type=F32)
        lane = lax.broadcasted_iota(jnp.int32, (96, 128), 1)
        prod[slot, 0:192, :] = full[:, 0:128]
        prod[slot, 192:288, :] = jnp.where(lane < 64, full[0:96, 128:256], full[96:192, 128:256])

    def wanted(i):
        return plane(8 + (1 - 2 * lax.rem(i, 2)) * lax.div(i + 1, 2))

    def finish_hess(both):
        pair = stk[192:384, pl.ds(pl.multiple_of(lax.div(z, 2) * 384, 128), 384)].astype(F32)
        pc = jnp.where(lax.rem(z, 2) == 0, pair[:, 0:192], pair[:, 192:384]) * (1.0 / TOKENS)
        at = jnp.transpose(both[0:192])
        bt = jnp.transpose(both[192:288])
        hess_ref[0:128, :] = pc[0:128] * at
        hess_ref[128:192, 0:96] = pc[128:192, 0:96] * bt[0:64]
        hess_ref[128:192, 96:192] = pc[128:192, 96:192] * bt[64:128]

    @pl.when(is_zero)
    def _():
        def hand(i, carry):
            product(wanted(i), i)
            send(prod.at[i], prod0.at[i], prod_send, prod_recv.at[i], z, other)
            return carry

        lax.fori_loop(0, NZ - 1, hand, 0)
        product(z, NZ - 1)
        wait_bytes(back.at[0], back_recv)
        finish_hess(back[0] + prod[NZ - 1])
        wait_bytes(prod.at[pl.ds(0, NZ - 1)], prod_send)

    @pl.when(is_one)
    def _():
        def rs_sub(w, n, s):
            return rs.at[(w * 9 + n) * 4 + s]

        def rs_take(w, n, s):
            wait_bytes(rs_sub(w, n, s), (rsr_recv if w == 0 else rsl_recv).at[(n - 1) * 4 + s])

        def rs_pass(w, n, s):
            sem = (rsr_recv if w == 0 else rsl_recv).at[n * 4 + s]
            send(rs_sub(w, n, s), rs_sub(w, n + 1, s), rs_send, sem, plane(1 - 2 * w), t)

        def own(i, s):
            lo = s % 2 * RSUB
            return (prod if s < 2 else prod0)[i, lo : lo + RSUB, :]

        def code(w, n, s, v):
            at = (w * 9 + n) * 4 + s
            high = v.astype(BF16)
            near = high.astype(F32)
            rest = jnp.where(jnp.abs(near) > 1e-30, (v - near) * pl.reciprocal(near, approx=True), 0.0)
            steps = jnp.round(rest * (1 / LOW))
            rs[at, 0:RSUB, :] = high
            rs[at, RSUB : RSUB + 64, :] = (21 * steps[0:64] + steps[80:RSUB]).astype(BF16)
            rs[at, RSUB + 64 : RMSG, :] = (21 * steps[64:80]).astype(BF16)

        def decode(w, n, s):
            at = (w * 9 + n) * 4 + s
            near = rs[at, 0:RSUB, :].astype(F32)
            low = rs[at, RSUB:RMSG, :].astype(F32)
            one = jnp.round(low * (1 / 21))
            two = low - 21 * one
            steps = jnp.concatenate([one, two[0:64]], axis=0)
            return near + near * (steps * LOW)

        def put(w, n, i, s, add):
            v = own(i, s)
            if add:
                rs_take(w, n, s)
                v = v + decode(w, n, s)
            code(w, n, s, v)
            rs_pass(w, n, s)

        def theirs(i):
            wait_bytes(prod0.at[i], prod_recv.at[i])

        product(wanted(0), 0)
        for s in (0, 1):
            put(0, 0, 0, s, False)
        theirs(0)
        for s in (2, 3):
            put(1, 0, 0, s, False)
        for n in range(1, 8):
            for w in range(2):
                product(wanted(2 * n - 1 + w), 2 * n - 1 + w)
            if n == 1:
                for s in (0, 1):
                    put(1, 1, 2, s, False)
                theirs(1)
                for s in (2, 3):
                    put(0, 1, 1, s, False)
                theirs(2)
                for s in (0, 1):
                    put(0, 1, 1, s, True)
                    put(1, 1, 2, s + 2, True)
                continue
            theirs(2 * n - 1)
            theirs(2 * n)
            for s in (2, 3, 0, 1):
                put(0, n, 2 * n - 1, s, True)
                put(1, n, 2 * n, s ^ 2, True)
        product(z, NZ - 1)
        for s in (2, 3):
            for w in range(2):
                rs_take(w, 8, s)
        back[1, 0:RSUB, :] = decode(0, 8, 2) + decode(1, 8, 2)
        back[1, RSUB:PK, :] = decode(0, 8, 3) + decode(1, 8, 3)
        send(back.at[1], back.at[0], back_send, back_recv, z, other)
        for s in (0, 1):
            for w in range(2):
                rs_take(w, 8, s)
        finish_hess(prod[NZ - 1] + jnp.concatenate([decode(0, 8, s) + decode(1, 8, s) for s in (0, 1)], axis=0))
        wait_bytes(back.at[0], back_send)
        wait_bytes(rs.at[pl.ds(0, 60)], rs_send)
        wait_bytes(pk.at[pl.ds(0, 15)], pk_send)
        wait_bytes(pk.at[pl.ds(0, 15), pl.ds(0, PK), :], w_send)

    rg_copy.wait()
    wait_bytes(ctx.at[pl.ds(0, 31 * BLK), :], ctx_send)

    @pl.when(is_zero)
    def _():
        wait_bytes(pk.at[0, pl.ds(0, PK), :], w_send)

    @pl.when(is_owner)
    def _():
        wait_bytes(mom.at[pl.ds(0, 7)], mom_send)
        wait_bytes(prod.at[0, pl.ds(0, 8 * (NT - 1)), :], cf_send)

    @pl.when(jnp.logical_not(is_owner))
    def _():
        wait_bytes(mom, mom_send)


def shards(context, residual, out_weight, norm_gain, norm_bias, target, probe):
    hbm = pl.BlockSpec(memory_space=pltpu.HBM)
    anywhere = pl.BlockSpec(memory_space=pl.ANY)
    vmem = pl.BlockSpec(memory_space=pltpu.VMEM)
    dma = pltpu.SemaphoreType.DMA
    arrays = (context, residual, out_weight, norm_gain.reshape(1, ROWS), norm_bias.reshape(1, ROWS), target, probe)
    arrays = [pltpu.with_memory_space_constraint(a, pltpu.HBM) for a in arrays]
    return pl.pallas_call(
        kernel,
        out_shape=(
            jax.ShapeDtypeStruct((ROWS, 192), F32),
            jax.ShapeDtypeStruct((ROWS, TOK), F32),
        ),
        in_specs=[hbm] * 7,
        out_specs=(vmem, anywhere),
        scratch_shapes=[
            pltpu.VMEM((NT * BLK, TOK), BF16),
            pltpu.VMEM((2 * ROWS, 3072), BF16),
            pltpu.VMEM((NZ, 2 * PK, 128), BF16),
            pltpu.VMEM((192, 192), BF16),
            pltpu.VMEM((ROWS, TOK), BF16),
            pltpu.VMEM((ROWS, TOK), BF16),
            pltpu.VMEM((ROWS, TOK), F32),
            pltpu.VMEM((ROWS, TOK), F32),
            pltpu.VMEM((1, ROWS), F32),
            pltpu.VMEM((1, ROWS), F32),
            pltpu.VMEM((ROWS, 128), F32),
            pltpu.VMEM((ROWS, 128), F32),
            pltpu.VMEM((8, 16, 128), F32),
            pltpu.VMEM((NT, 16, 128), F32),
            pltpu.VMEM((8, 8, 128), F32),
            pltpu.VMEM((256, 128), F32),
            pltpu.VMEM((TOK, 256), BF16),
            pltpu.VMEM((ROWS, TOK), F32),
            pltpu.VMEM((18 * 4, RMSG, 128), BF16),
            pltpu.VMEM((NZ, PK, 128), F32),
            pltpu.VMEM((NZ, PK, 128), F32),
            pltpu.VMEM((2, PK, 128), F32),
            dma((8,)),
            dma,
            dma((4,)),
            dma((24,)),
            dma((16,)),
            dma,
            dma((24,)),
            dma((24,)),
            dma,
            dma((16,)),
            dma,
            dma,
            dma,
            dma((8,)),
            dma,
            dma((32,)),
            dma((32,)),
            dma,
            dma((16,)),
            dma,
            dma,
        ],
        compiler_params=pltpu.CompilerParams(
            collective_id=0, has_side_effects=True, vmem_limit_bytes=48 * 1024 * 1024
        ),
    )(*arrays)


def solution(mesh):
    return jax.shard_map(
        shards,
        mesh=mesh,
        in_specs=(
            P("tensor", "dp"),
            P("tensor", "dp"),
            P("tensor", "dp"),
            P("tensor"),
            P("tensor"),
            P("tensor", "dp"),
            P("tensor", None),
        ),
        out_specs=(P("tensor", "dp"), P("tensor", "dp")),
        check_vma=False,
    )
```

```python
import jax
import jax.numpy as jnp
from jax import lax
from jax.experimental import pallas as pl
from jax.experimental.pallas import tpu as pltpu
from jax.sharding import PartitionSpec as P

MESH = pl.DeviceIdType.MESH
F32 = jnp.float32
BF16 = jnp.bfloat16

D = 6144
ROWS = 192
TOK = 1024
BLK = 96
NZ = 16
NT = 32
PK = 288
ZSUB = 192
RSUB = 144
RMSG = 224
LOW = 2.0**-8 / 10
GROUPS = ((0, 1), (1, 2), (2, 3), (3, 5), (5, 7), (7, 15))
FAST = 2 * 3
TOKENS = 16384

PLAN = (
    (
        ("S", "Q0"), ("S", "P"), ("W", "P"), ("W", "Q0"), ("S", "QQ0"), ("S", "cP"), ("S", "Q1"), ("S", "P2"),
        ("W", "QQ0"), ("W", "P2"), ("S", "cQ0"), ("S", "QA"), ("S", "QB"), ("W", "Q1"), ("S", "QQ1"), ("W", "QA"),
        ("S", "cP2"), ("S", "QQ2"), ("S", "cQQ0"), ("W", "QB"), ("S", "cQ1"), ("S", "cQ2"), ("W", "QQ1"),
        ("S", "cQQ1"), ("W", "QQ2"), ("S", "cQQ2"), ("S", "cO"),
    ),
    (
        ("S", "z", 1, 1), ("S", "P"), ("S", "Q0"), ("S", "z", 2, 0), ("S", "cO"), ("S", "z", 2, 1), ("W", "z", 1, 1),
        ("S", "z", 2, 2), ("S", "z", 1, 0), ("W", "P"), ("S", "P2"), ("S", "z", 1, 2), ("W", "z", 2, 0),
        ("S", "z", 4, 0), ("W", "z", 2, 1), ("S", "Q1"), ("S", "z", 4, 1), ("W", "z", 2, 2), ("S", "z", 3, 2),
        ("W", "Q0"), ("S", "QQ0"), ("S", "z", 4, 2), ("S", "z", 3, 0), ("W", "z", 4, 0), ("S", "z", 6, 0),
        ("W", "P2"), ("W", "z", 4, 1), ("S", "z", 3, 1), ("S", "z", 6, 1), ("S", "cP"), ("S", "QA"), ("W", "z", 3, 2),
        ("W", "z", 4, 2), ("S", "z", 6, 2), ("S", "QB"), ("W", "z", 1, 2), ("W", "Q1"), ("S", "cz", 2), ("S", "cQ1"),
        ("S", "cQ0"), ("W", "z", 6, 0), ("W", "z", 1, 0), ("S", "z", 7, 0), ("S", "QQ1"), ("W", "z", 3, 1),
        ("S", "z", 5, 2), ("S", "z", 5, 0), ("W", "z", 6, 1), ("S", "z", 7, 1), ("S", "cP2"), ("W", "QB"),
        ("W", "QA"), ("W", "z", 6, 2), ("S", "z", 7, 2), ("S", "QQ2"), ("S", "cQ2"), ("S", "cz", 4), ("W", "z", 7, 0),
        ("S", "z", 5, 1), ("S", "cz", 1), ("S", "cz", 6), ("S", "z", 8, 0), ("W", "z", 7, 1), ("S", "z", 8, 1),
        ("W", "QQ1"), ("S", "cz", 3), ("W", "z", 3, 0), ("W", "z", 7, 2), ("S", "z", 8, 2), ("S", "cQQ1"),
        ("S", "cz", 7), ("W", "QQ0"), ("W", "QQ2"), ("W", "z", 5, 1), ("S", "cQQ0"), ("W", "z", 5, 2), ("S", "cz", 5),
        ("W", "z", 8, 1), ("W", "z", 8, 0), ("S", "cQQ2"), ("W", "z", 5, 0), ("W", "z", 8, 2), ("S", "cz", 8),
    ),
)
SENDS = {
    "P": (((0, 0), None, (1, 0)), ((0, 0), None, (-1, 0))),
    "P2": (((-1, 0), 0, (1, 0)), ((1, 0), 1, (-1, 0))),
    "Q0": (((0, 0), None, (0, 1)), ((0, 0), None, (0, -1))),
    "Q1": tuple(((a, 0), None, (0, b)) for a in (-1, 1) for b in (1, -1)),
    "QA": (((2, 0), 0, (0, 1)), ((2, 0), 1, (0, -1))),
    "QB": (((2, 0), 0, (0, -1)), ((2, 0), 1, (0, 1))),
    "QQ0": (((0, -1), 0, (0, 1)), ((0, 1), 1, (0, -1))),
    "QQ1": tuple(((a, -b), (1 - b) // 2, (0, b)) for a in (-1, 1) for b in (1, -1)),
    "QQ2": (((2, -1), 0, (0, 1)), ((2, 1), 1, (0, -1))),
}
NAMES = tuple(SENDS)
BLOCKS = {"P": 2, "P2": 1, "Q0": 2, "Q1": 4, "QA": 1, "QB": 1, "QQ0": 1, "QQ1": 2, "QQ2": 1}
CORE = {
    "cO": ((0, 0),),
    "cP": ((-1, 0), (1, 0)),
    "cP2": ((2, 0),),
    "cQ0": ((0, -1), (0, 1)),
    "cQ1": ((-1, -1), (-1, 1), (1, -1), (1, 1)),
    "cQ2": ((2, -1), (2, 1)),
    "cQQ0": ((0, 2),),
    "cQQ1": ((-1, 2), (1, 2)),
    "cQQ2": ((2, 2),),
}


def kernel(
    ctx_in, res_in, w_in, gain_in, bias_in, tgt_in, probe_in,
    hess_ref, rg_out,
    ctx, stk, pk, wloc, res, tgt, xv, tau, grow, brow, gainb, biasb, mom, mbuf, cbuf, curv, curvt, rg, rs, early, prod, prod0,
    load_sem, ctx_send, g_recv, c_recv, pk_send, pk_recv, w_send, w_recv,
    mom_send, mom_recv, cf_send, cf_recv, rs_send, rs_recv, prod_send, prod_recv,
):
    z = lax.axis_index("dp")
    t = lax.axis_index("tensor")
    core = lax.rem(t, 2)
    x = lax.div(t, 8)
    y = lax.rem(lax.div(t, 2), 4)
    other = t + 1 - 2 * core
    is_one = core == 1
    is_zero = core == 0

    def plane(n):
        return lax.rem(z + n + NZ, NZ)


    def wait_bytes(ref, sem):
        pltpu.make_async_copy(ref, ref, sem).wait()

    def send(src, dst, ssem, rsem, zz, tt):
        pltpu.make_async_remote_copy(
            src_ref=src, dst_ref=dst, send_sem=ssem, recv_sem=rsem, device_id=(zz, tt), device_id_type=MESH
        ).start()

    barrier = pltpu.get_barrier_semaphore()
    for n in (1, -1, 2, -2):
        pl.semaphore_signal(barrier, inc=1, device_id=(plane(n), t), device_id_type=MESH)
    for n in (1, -1):
        pl.semaphore_signal(barrier, inc=1, device_id=(plane(n), other), device_id_type=MESH)

    def greet(i, carry):
        pl.semaphore_signal(barrier, inc=1, device_id=(z, lax.rem(t + i, NT)), device_id_type=MESH)
        return carry

    lax.fori_loop(1, NT, greet, 0)

    own_rows = pl.ds(pl.multiple_of(t * BLK, 32), BLK)
    own = ctx.at[own_rows, :]
    loads = [
        pltpu.make_async_copy(w_in, wloc, load_sem.at[0]),
        pltpu.make_async_copy(probe_in, stk.at[pl.ds(ROWS, ROWS), :], load_sem.at[1]),
        pltpu.make_async_copy(ctx_in, own, load_sem.at[2]),
        pltpu.make_async_copy(res_in, res, load_sem.at[3]),
        pltpu.make_async_copy(tgt_in, tgt, load_sem.at[4]),
        pltpu.make_async_copy(gain_in, grow, load_sem.at[6]),
        pltpu.make_async_copy(bias_in, brow, load_sem.at[7]),
    ]
    for c in loads:
        c.start()
    loads[0].wait()
    half_at = pl.multiple_of((1 - core) * PK, 32)
    pk[z, pl.ds(half_at, 192), :] = wloc[:, 0:128]
    pk[z, pl.ds(half_at + 192, 96), 0:64] = wloc[0:96, 128:192]
    pk[z, pl.ds(half_at + 192, 96), 64:128] = wloc[96:192, 128:192]
    pl.semaphore_wait(barrier, NT + 5)

    def zero_half(j):
        return pk.at[j, pl.ds(PK, PK), :]

    def pk_sub(j, s):
        return pk.at[j, pl.ds(s * ZSUB, ZSUB), :]

    def gather(c):
        p, q = (y, x) if c else (x, y)
        sp, sq = (2, 8) if c else (8, 2)

        def dev(dp, dq):
            return lax.rem(p + dp + 4, 4) * sp + lax.rem(q + dq + 4, 4) * sq + c

        def rows_of(dp, dq):
            return pl.ds(pl.multiple_of(dev(dp, dq) * BLK, 32), BLK)

        def blk(dp, dq, half=None):
            rows = rows_of(dp, dq)
            return ctx.at[rows, :] if half is None else ctx.at[rows, pl.ds(half * 512, 512)]

        if c == 0:
            send(zero_half(z), zero_half(z), w_send, w_recv, z, other)
        waited = False
        for act, name, *ab in PLAN[c]:
            if name == "cz":
                for sign in (1, -1)[: 1 if ab[0] == 8 else 2]:
                    ref = zero_half(plane(sign * ab[0]))
                    send(ref, ref, w_send, w_recv, z, other)
            elif name in CORE:
                for at in CORE[name]:
                    src = ctx_in if name == "cO" else blk(*at)
                    send(src, blk(*at), ctx_send, c_recv, z, other)
            elif name == "z":
                n, part = ab
                sem = pk_recv.at[(n - 1) * 3 + part]
                signs = (1, -1) if n < 8 else (1,) if part < 2 else (-1,)
                if act == "W":
                    wait_bytes(pk.at[pl.ds(0, len(signs)), pl.ds(0, ZSUB), :], sem)
                    continue
                hop = 2 if n <= FAST and n % 2 == 0 else 1
                if n == hop and not waited:
                    waited = True
                    wait_bytes(zero_half(z), w_recv)
                for sign in signs:
                    ref = pk_sub(plane(sign * (hop - n)), part)
                    send(ref, ref, pk_send, sem, plane(sign * hop), t)
            elif act == "S":
                for at, half, to in SENDS[name]:
                    dst = blk(*at, half)
                    send(ctx_in if at == (0, 0) else dst, dst, ctx_send, g_recv.at[NAMES.index(name)], z, dev(*to))
            else:
                wait_bytes(ctx.at[pl.ds(0, BLOCKS[name] * BLK), :], g_recv.at[NAMES.index(name)])
        if c == 0:
            wait_bytes(pk.at[pl.ds(0, NZ - 1), pl.ds(0, PK), :], w_recv)

    @pl.when(is_zero)
    def _():
        gather(0)

    @pl.when(is_one)
    def _():
        gather(1)

    for c in loads[5:]:
        c.wait()
    gainb[...] = jnp.transpose(jnp.broadcast_to(grow[...], (128, ROWS)))
    biasb[...] = jnp.transpose(jnp.broadcast_to(brow[...], (128, ROWS)))
    for j in range(NZ):
        c = 192 * j
        stk[0:192, c : c + 128] = pk[j, pl.ds(half_at, 192), :]
        stk[0:96, c + 128 : c + 192] = pk[j, pl.ds(half_at + 192, 96), 0:64]
        stk[96:192, c + 128 : c + 192] = pk[j, pl.ds(half_at + 192, 96), 64:128]
    wait_bytes(ctx.at[pl.ds(0, 16 * BLK), :], c_recv)
    for c in loads[1:5]:
        c.wait()

    for n in range(2):
        cols = slice(n * 512, (n + 1) * 512)
        both = jnp.dot(stk[...], ctx[:, cols], preferred_element_type=F32)
        xv[:, cols] = both[0:192]
        tau[:, cols] = both[192:384]

    def sums(i, carry):
        k = lax.rem(2 * x + 4 + i, 8)
        lanes = pl.ds(pl.multiple_of(k * 128, 128), 128)
        tot = jnp.zeros((16, 128), F32)
        for r in range(12):
            rows = pl.ds(r * 16, 16)
            xx = xv[rows, lanes] + res[rows, lanes].astype(F32)
            xv[rows, lanes] = xx
            tot = tot + xx
        mean = jnp.sum(tot, axis=0, keepdims=True) / ROWS
        accs = [jnp.zeros((16, 128), F32) for _ in range(11)]
        for r in range(12):
            rows = pl.ds(r * 16, 16)
            yy = xv[rows, lanes] - mean
            tt = tau[rows, lanes]
            g = gainb[rows, :]
            w = g * g
            h = g * (biasb[rows, :] - tgt[rows, lanes].astype(F32))
            wy = w * yy
            wt = w * tt
            terms = (yy * yy, wy, wy * yy, h, h * yy, tt, yy * tt, wt, wy * tt, h * tt, w)
            accs = [a + b for a, b in zip(accs, terms)]
        mom[k, 0:1, :] = mean
        for a in range(11):
            mom[k, a + 1 : a + 2, :] = jnp.sum(accs[a], axis=0, keepdims=True)
        mom[k, 12:16, :] = jnp.ones((4, 128), F32)

        @pl.when(t != 4 * k + 1)
        def _():
            send(mom.at[k], mbuf.at[t], mom_send, mom_recv, z, 4 * k + 1)

        return carry

    lax.fori_loop(0, 8, sums, 0)
    mine = lax.div(t, 4)
    is_owner = lax.rem(t, 4) == 1

    @pl.when(is_owner)
    def _():
        mbuf[t] = mom[mine]
        wait_bytes(mbuf.at[pl.ds(0, NT - 1)], mom_recv)
        s0 = mbuf[0]
        for i in range(1, NT):
            s0 = s0 + mbuf[i]
        mean = s0[0:1] / NT
        s1 = jnp.zeros((16, 128), F32)
        s2 = jnp.zeros((16, 128), F32)
        for i in range(NT):
            m = mbuf[i]
            dm = (m[0:1] - mean) * m
            s1 = s1 + dm
            s2 = s2 + (m[0:1] - mean) * dm

        def row(a, i):
            return a[i : i + 1]

        s_w = row(s0, 11)
        s_h = row(s0, 4)
        s_t = row(s0, 6)
        s_wt = row(s0, 8)
        s_ht = row(s0, 10)
        s_zz = row(s0, 1) + ROWS * row(s2, 12)
        s_wz = row(s0, 2) + row(s1, 11)
        s_wzz = row(s0, 3) + 2 * row(s1, 2) + row(s2, 11)
        s_hz = row(s0, 5) + row(s1, 4)
        s_zt = row(s0, 7) + row(s1, 6)
        s_wzt = row(s0, 9) + row(s1, 8)
        sc = 1.0 / jnp.sqrt(s_zz / D + 1e-05)
        s_wn = sc * s_wz
        s_wnn = sc * sc * s_wzz
        s_hn = sc * s_hz
        g_mean = (s_wn + s_h) / D
        g_proj = (s_wnn + s_hn) / D
        t_mean = s_t / D
        t_proj = sc * s_zt / D
        c_mean = sc * (s_wt - t_mean * s_w - t_proj * s_wn) / D
        c_proj = sc * (2 * (sc * s_wzt - t_mean * s_wn - t_proj * s_wnn) + s_ht - t_mean * s_h - t_proj * s_hn) / D
        for i, v in enumerate((mean, sc, g_mean, g_proj, t_mean, t_proj, c_mean, c_proj)):
            cbuf[mine, i : i + 1, :] = v

        steps = sorted(((dx, dy) for dx in range(4) for dy in range(4)), key=lambda d: -min(d[0], 4 - d[0]) - min(d[1], 4 - d[1]))
        for dx, dy in steps:
            chip = lax.rem(x + dx, 4) * 8 + lax.rem(y + dy, 4) * 2
            for c in (0, 1):
                if (dx, dy, c) != (0, 0, 1):
                    send(cbuf.at[mine], cbuf.at[mine], cf_send, cf_recv.at[mine], z, chip + c)

    def finish(i, carry):
        k = lax.rem(2 * x + 6 + i, 8)

        @pl.when(t != 4 * k + 1)
        def _():
            wait_bytes(cbuf.at[k], cf_recv.at[k])

        lanes = pl.ds(pl.multiple_of(k * 128, 128), 128)
        mean, sc, g_mean, g_proj, t_mean, t_proj, c_mean, c_proj = [cbuf[k, a : a + 1, :] for a in range(8)]
        lead = -sc * t_proj
        for r in range(12):
            rows = pl.ds(r * 16, 16)
            n = (xv[rows, lanes] - mean) * sc
            g = gainb[rows, :]
            w = g * g
            gn = g * (g * n + biasb[rows, :] - tgt[rows, lanes].astype(F32))
            grad = sc * (gn - g_mean - n * g_proj)
            rg[rows, lanes] = grad
            u = sc * (tau[rows, lanes] - t_mean - n * t_proj)
            cv = lead * grad + sc * (w * u - c_mean - u * g_proj - n * c_proj)
            curv[rows, :] = cv
            if r >= 8:
                curv[pl.ds(r * 16 + 64, 16), :] = cv
        curvt[pl.ds(pl.multiple_of(k * 128, 128), 128), :] = jnp.transpose(curv[...]).astype(BF16)
        return carry

    lax.fori_loop(0, 8, finish, 0)
    rg_copy = pltpu.make_async_copy(rg, rg_out, load_sem.at[5])
    rg_copy.start()

    lane = lax.broadcasted_iota(jnp.int32, (96, 128), 1)

    def pack(full, to, slot):
        to[slot, 0:192, :] = full[:, 0:128]
        to[slot, 192:288, :] = jnp.where(lane < 64, full[0:96, 128:256], full[96:192, 128:256])

    def product(i, to, slot):
        rows = pl.ds(pl.multiple_of(wanted(i) * 192, 64), 192)
        pack(jnp.dot(ctx[rows, :], curvt[...], preferred_element_type=F32), to, slot)

    def products():
        for b in range(4):
            full = jnp.dot(ctx[768 * b : 768 * (b + 1), :], curvt[...], preferred_element_type=F32)
            for i in range(4):
                pack(full[192 * i : 192 * (i + 1)], prod, 4 * b + i)

    def wanted(i):
        return plane(8 + (1 - 2 * lax.rem(i, 2)) * lax.div(i + 1, 2))

    def finish_hess(both):
        pair = stk[192:384, pl.ds(pl.multiple_of(lax.div(z, 2) * 384, 128), 384)].astype(F32)
        pc = jnp.where(lax.rem(z, 2) == 0, pair[:, 0:192], pair[:, 192:384]) * (1.0 / TOKENS)
        at = jnp.transpose(both[0:192])
        bt = jnp.transpose(both[192:288])
        hess_ref[0:128, :] = pc[0:128] * at
        hess_ref[128:192, 0:96] = pc[128:192, 0:96] * bt[0:64]
        hess_ref[128:192, 96:192] = pc[128:192, 96:192] * bt[64:128]

    def rs_sub(w, n, s):
        return rs.at[(w * 9 + n) * 4 + s]

    def rs_sem(w, n, s):
        return rs_recv.at[(w * 8 + n - 1) * 4 + s]

    def rs_take(w, n, s):
        wait_bytes(rs_sub(w, n, s), rs_sem(w, n, s))

    def decode(w, n, s):
        at = (w * 9 + n) * 4 + s
        near = rs[at, 0:RSUB, :].astype(F32)
        low = rs[at, RSUB:RMSG, :].astype(F32)
        one = jnp.round(low * (1 / 21))
        two = low - 21 * one
        steps = jnp.concatenate([one, two[0:64]], axis=0)
        return near + near * (steps * LOW)

    def last_of(first):
        parts = []
        for s in (first, first + 1):
            for w in range(2):
                rs_take(w, 8, s)
            parts.append(decode(0, 8, s) + decode(1, 8, s))
        finish_hess(prod[z] + jnp.concatenate(parts, axis=0))

    @pl.when(is_zero)
    def _():
        for group, (lo, hi) in enumerate(GROUPS):

            def hand(i, carry, group=group):
                product(i, prod, wanted(i))
                send(prod.at[wanted(i)], prod0.at[i], prod_send, prod_recv.at[group], z, other)
                return carry

            lax.fori_loop(lo, hi, hand, 0)
        product(NZ - 1, prod, z)
        last_of(2)
        wait_bytes(prod.at[pl.ds(0, NZ - 1)], prod_send)

    @pl.when(is_one)
    def _():
        def rs_pass(w, n, s):
            to = other if n == 7 and s > 1 else t
            send(rs_sub(w, n, s), rs_sub(w, n + 1, s), rs_send, rs_sem(w, n + 1, s), plane(1 - 2 * w), to)

        def own(i, s):
            lo = s % 2 * RSUB
            if s > 1:
                return prod0[i, lo : lo + RSUB, :]
            return early[i // 2, lo : lo + RSUB, :] if i in (0, 2) else prod[wanted(i), lo : lo + RSUB, :]

        def code(w, n, s, v):
            at = (w * 9 + n) * 4 + s
            high = v.astype(BF16)
            near = high.astype(F32)
            rest = jnp.where(jnp.abs(near) > 1e-30, (v - near) * pl.reciprocal(near, approx=True), 0.0)
            steps = jnp.round(rest * (1 / LOW))
            rs[at, 0:RSUB, :] = high
            rs[at, RSUB : RSUB + 64, :] = (21 * steps[0:64] + steps[80:RSUB]).astype(BF16)
            rs[at, RSUB + 64 : RMSG, :] = (21 * steps[64:80]).astype(BF16)

        def put(w, n, i, s, add):
            v = own(i, s)
            if add:
                rs_take(w, n, s)
                v = v + decode(w, n, s)
            code(w, n, s, v)
            rs_pass(w, n, s)

        def theirs(group):
            lo, hi = GROUPS[group]
            wait_bytes(prod0.at[pl.ds(lo, hi - lo)], prod_recv.at[group])

        product(0, early, 0)
        for s in (0, 1):
            put(0, 0, 0, s, False)
        theirs(0)
        for s in (2, 3):
            put(1, 0, 0, s, False)
        product(2, early, 1)
        for s in (0, 1):
            put(1, 1, 2, s, False)
        theirs(1)
        for s in (2, 3):
            put(0, 1, 1, s, False)
        products()
        theirs(2)
        for s in (0, 1):
            put(0, 1, 1, s, True)
            put(1, 1, 2, s + 2, True)
        for n in range(2, 8):
            if n < 5:
                theirs(n + 1)
            for s in (2, 3, 0, 1):
                put(0, n, 2 * n - 1, s, True)
                put(1, n, 2 * n, s ^ 2, True)
        last_of(0)
        wait_bytes(rs.at[pl.ds(0, 60)], rs_send)
        wait_bytes(pk.at[pl.ds(0, 15)], pk_send)
        wait_bytes(pk.at[pl.ds(0, 15), pl.ds(0, PK), :], w_send)

    rg_copy.wait()
    wait_bytes(ctx.at[pl.ds(0, 31 * BLK), :], ctx_send)

    @pl.when(is_zero)
    def _():
        wait_bytes(pk.at[0, pl.ds(0, PK), :], w_send)

    @pl.when(is_owner)
    def _():
        wait_bytes(mom.at[pl.ds(0, 7)], mom_send)
        wait_bytes(prod.at[0, pl.ds(0, 8 * (NT - 1)), :], cf_send)

    @pl.when(jnp.logical_not(is_owner))
    def _():
        wait_bytes(mom, mom_send)


def shards(context, residual, out_weight, norm_gain, norm_bias, target, probe):
    hbm = pl.BlockSpec(memory_space=pltpu.HBM)
    anywhere = pl.BlockSpec(memory_space=pl.ANY)
    vmem = pl.BlockSpec(memory_space=pltpu.VMEM)
    dma = pltpu.SemaphoreType.DMA
    arrays = (context, residual, out_weight, norm_gain.reshape(1, ROWS), norm_bias.reshape(1, ROWS), target, probe)
    arrays = [pltpu.with_memory_space_constraint(a, pltpu.HBM) for a in arrays]
    return pl.pallas_call(
        kernel,
        out_shape=(
            jax.ShapeDtypeStruct((ROWS, 192), F32),
            jax.ShapeDtypeStruct((ROWS, TOK), F32),
        ),
        in_specs=[hbm] * 7,
        out_specs=(vmem, anywhere),
        scratch_shapes=[
            pltpu.VMEM((NT * BLK, TOK), BF16),
            pltpu.VMEM((2 * ROWS, 3072), BF16),
            pltpu.VMEM((NZ, 2 * PK, 128), BF16),
            pltpu.VMEM((192, 192), BF16),
            pltpu.VMEM((ROWS, TOK), BF16),
            pltpu.VMEM((ROWS, TOK), BF16),
            pltpu.VMEM((ROWS, TOK), F32),
            pltpu.VMEM((ROWS, TOK), F32),
            pltpu.VMEM((1, ROWS), F32),
            pltpu.VMEM((1, ROWS), F32),
            pltpu.VMEM((ROWS, 128), F32),
            pltpu.VMEM((ROWS, 128), F32),
            pltpu.VMEM((8, 16, 128), F32),
            pltpu.VMEM((NT, 16, 128), F32),
            pltpu.VMEM((8, 8, 128), F32),
            pltpu.VMEM((256, 128), F32),
            pltpu.VMEM((TOK, 256), BF16),
            pltpu.VMEM((ROWS, TOK), F32),
            pltpu.VMEM((18 * 4, RMSG, 128), BF16),
            pltpu.VMEM((2, PK, 128), F32),
            pltpu.VMEM((NZ, PK, 128), F32),
            pltpu.VMEM((NZ, PK, 128), F32),
            dma((8,)),
            dma,
            dma((9,)),
            dma,
            dma,
            dma((24,)),
            dma,
            dma,
            dma,
            dma,
            dma,
            dma((8,)),
            dma,
            dma((64,)),
            dma,
            dma((len(GROUPS),)),
        ],
        compiler_params=pltpu.CompilerParams(
            collective_id=0, has_side_effects=True, vmem_limit_bytes=48 * 1024 * 1024
        ),
    )(*arrays)


def solution(mesh):
    return jax.shard_map(
        shards,
        mesh=mesh,
        in_specs=(
            P("tensor", "dp"),
            P("tensor", "dp"),
            P("tensor", "dp"),
            P("tensor"),
            P("tensor"),
            P("tensor", "dp"),
            P("tensor", None),
        ),
        out_specs=(P("tensor", "dp"), P("tensor", "dp")),
        check_vma=False,
    )
```

```python
import jax
import jax.numpy as jnp
from jax import lax
from jax.experimental import pallas as pl
from jax.experimental.pallas import tpu as pltpu
from jax.sharding import PartitionSpec as P

MESH = pl.DeviceIdType.MESH
F32 = jnp.float32
BF16 = jnp.bfloat16

D = 6144
ROWS = 192
TOK = 1024
BLK = 96
NZ = 16
NT = 32
PK = 288
ZSUB = 192
RSUB = 144
RMSG = 224
LOW = 2.0**-8 / 10
GROUPS = ((0, 1), (1, 2), (2, 3), (3, 5), (5, 7), (7, 15))
FAST = 2 * 3
TOKENS = 16384

PLAN = (
    (
        ("S", "cO"), ("S", "P"), ("S", "Q0"), ("W", "P"), ("S", "Q1"), ("S", "P2"), ("W", "P2"), ("S", "QA"),
        ("S", "cP2"), ("S", "cP"), ("W", "Q0"), ("S", "QQ0"), ("S", "QB"), ("W", "Q1"), ("S", "QQ1"), ("S", "cQ0"),
        ("W", "QA"), ("S", "QQ2"), ("S", "cQ1"), ("W", "QB"), ("W", "QQ0"), ("S", "cQ2"), ("W", "QQ1"), ("S", "cQQ1"),
        ("S", "cQQ0"), ("W", "QQ2"), ("S", "cQQ2"),
    ),
    (
        ("S", "P"), ("S", "z", 2, 0), ("S", "z", 2, 1), ("S", "cO"), ("S", "z", 2, 2), ("S", "z", 1, 2),
        ("W", "z", 2, 0), ("S", "Q0"), ("S", "z", 4, 0), ("W", "z", 1, 2), ("S", "z", 1, 1), ("S", "z", 1, 0),
        ("W", "P"), ("S", "P2"), ("W", "z", 2, 1), ("S", "z", 4, 1), ("W", "z", 2, 2), ("S", "Q1"), ("W", "z", 4, 0),
        ("S", "z", 4, 2), ("W", "z", 1, 0), ("S", "z", 3, 2), ("S", "z", 6, 0), ("W", "z", 1, 1), ("W", "z", 4, 1),
        ("S", "cz", 2), ("S", "z", 6, 1), ("W", "Q0"), ("S", "cP"), ("W", "P2"), ("S", "z", 3, 1), ("S", "QA"),
        ("W", "z", 4, 2), ("S", "z", 6, 2), ("S", "cP2"), ("S", "QB"), ("W", "z", 6, 0), ("S", "QQ0"),
        ("S", "z", 7, 0), ("S", "cz", 4), ("W", "Q1"), ("S", "z", 5, 1), ("S", "cQ1"), ("W", "z", 6, 1),
        ("S", "z", 7, 1), ("S", "QQ1"), ("S", "cQ0"), ("S", "z", 5, 0), ("W", "z", 3, 1), ("W", "z", 6, 2),
        ("S", "z", 7, 2), ("S", "cz", 1), ("W", "QB"), ("W", "QA"), ("W", "z", 5, 1), ("S", "z", 3, 0),
        ("S", "z", 5, 2), ("S", "cQ2"), ("W", "z", 3, 2), ("W", "z", 7, 1), ("S", "cz", 6), ("S", "QQ2"),
        ("S", "cz", 3), ("W", "z", 7, 0), ("S", "z", 8, 1), ("W", "z", 5, 0), ("W", "QQ0"), ("W", "z", 7, 2),
        ("S", "z", 8, 2), ("S", "cQQ0"), ("S", "cz", 7), ("W", "QQ1"), ("S", "z", 8, 0), ("S", "cQQ1"),
        ("W", "z", 5, 2), ("S", "cz", 5), ("W", "z", 8, 1), ("W", "QQ2"), ("S", "cQQ2"), ("W", "z", 8, 2),
        ("S", "cz", 8), ("W", "z", 3, 0), ("W", "z", 8, 0),
    ),
)
SENDS = {
    "P": (((0, 0), None, (1, 0)), ((0, 0), None, (-1, 0))),
    "P2": (((-1, 0), 0, (1, 0)), ((1, 0), 1, (-1, 0))),
    "Q0": (((0, 0), None, (0, 1)), ((0, 0), None, (0, -1))),
    "Q1": tuple(((a, 0), None, (0, b)) for a in (-1, 1) for b in (1, -1)),
    "QA": (((2, 0), 0, (0, 1)), ((2, 0), 1, (0, -1))),
    "QB": (((2, 0), 0, (0, -1)), ((2, 0), 1, (0, 1))),
    "QQ0": (((0, -1), 0, (0, 1)), ((0, 1), 1, (0, -1))),
    "QQ1": tuple(((a, -b), (1 - b) // 2, (0, b)) for a in (-1, 1) for b in (1, -1)),
    "QQ2": (((2, -1), 0, (0, 1)), ((2, 1), 1, (0, -1))),
}
NAMES = tuple(SENDS)
BLOCKS = {"P": 2, "P2": 1, "Q0": 2, "Q1": 4, "QA": 1, "QB": 1, "QQ0": 1, "QQ1": 2, "QQ2": 1}
CORE = {
    "cO": ((0, 0),),
    "cP": ((-1, 0), (1, 0)),
    "cP2": ((2, 0),),
    "cQ0": ((0, -1), (0, 1)),
    "cQ1": ((-1, -1), (-1, 1), (1, -1), (1, 1)),
    "cQ2": ((2, -1), (2, 1)),
    "cQQ0": ((0, 2),),
    "cQQ1": ((-1, 2), (1, 2)),
    "cQQ2": ((2, 2),),
}


def kernel(
    ctx_in, res_in, w_in, gain_in, bias_in, tgt_in, probe_in,
    hess_ref, rg_out,
    ctx, stk, pk, wloc, res, tgt, xv, tau, grow, brow, gainb, biasb, mom, mbuf, cbuf, curv, curvt, rg, rs, early, prod, prod0,
    load_sem, ctx_send, g_recv, c_recv, pk_send, pk_recv, w_send, w_recv,
    mom_send, mom_recv, cf_send, cf_recv, rs_send, rs_recv, prod_send, prod_recv,
):
    z = lax.axis_index("dp")
    t = lax.axis_index("tensor")
    core = lax.rem(t, 2)
    x = lax.div(t, 8)
    y = lax.rem(lax.div(t, 2), 4)
    other = t + 1 - 2 * core
    is_one = core == 1
    is_zero = core == 0

    def plane(n):
        return lax.rem(z + n + NZ, NZ)


    def wait_bytes(ref, sem):
        pltpu.make_async_copy(ref, ref, sem).wait()

    def send(src, dst, ssem, rsem, zz, tt):
        pltpu.make_async_remote_copy(
            src_ref=src, dst_ref=dst, send_sem=ssem, recv_sem=rsem, device_id=(zz, tt), device_id_type=MESH
        ).start()

    barrier = pltpu.get_barrier_semaphore()
    for n in (1, -1, 2, -2):
        pl.semaphore_signal(barrier, inc=1, device_id=(plane(n), t), device_id_type=MESH)
    for n in (1, -1):
        pl.semaphore_signal(barrier, inc=1, device_id=(plane(n), other), device_id_type=MESH)

    def greet(i, carry):
        pl.semaphore_signal(barrier, inc=1, device_id=(z, lax.rem(t + i, NT)), device_id_type=MESH)
        return carry

    lax.fori_loop(1, NT, greet, 0)

    own_rows = pl.ds(pl.multiple_of(t * BLK, 32), BLK)
    own = ctx.at[own_rows, :]
    loads = [
        pltpu.make_async_copy(w_in, wloc, load_sem.at[0]),
        pltpu.make_async_copy(probe_in, stk.at[pl.ds(ROWS, ROWS), :], load_sem.at[1]),
        pltpu.make_async_copy(ctx_in, own, load_sem.at[2]),
        pltpu.make_async_copy(res_in, res, load_sem.at[3]),
        pltpu.make_async_copy(tgt_in, tgt, load_sem.at[4]),
        pltpu.make_async_copy(gain_in, grow, load_sem.at[6]),
        pltpu.make_async_copy(bias_in, brow, load_sem.at[7]),
    ]
    for c in loads:
        c.start()
    pl.semaphore_wait(barrier, NT + 5)

    half_at = pl.multiple_of((1 - core) * PK, 32)

    def pack_weight():
        loads[0].wait()
        pk[z, pl.ds(half_at, 192), :] = wloc[:, 0:128]
        pk[z, pl.ds(half_at + 192, 96), 0:64] = wloc[0:96, 128:192]
        pk[z, pl.ds(half_at + 192, 96), 64:128] = wloc[96:192, 128:192]

    def zero_half(j):
        return pk.at[j, pl.ds(PK, PK), :]

    def pk_sub(j, s):
        return pk.at[j, pl.ds(s * ZSUB, ZSUB), :]

    def gather(c):
        p, q = (y, x) if c else (x, y)
        sp, sq = (2, 8) if c else (8, 2)

        def dev(dp, dq):
            return lax.rem(p + dp + 4, 4) * sp + lax.rem(q + dq + 4, 4) * sq + c

        def rows_of(dp, dq):
            return pl.ds(pl.multiple_of(dev(dp, dq) * BLK, 32), BLK)

        def blk(dp, dq, half=None):
            rows = rows_of(dp, dq)
            return ctx.at[rows, :] if half is None else ctx.at[rows, pl.ds(half * 512, 512)]

        packed = waited = False
        for act, name, *ab in PLAN[c]:
            if not packed and (act == "W" or name == "z"):
                packed = True
                pack_weight()
                if c == 0:
                    send(zero_half(z), zero_half(z), w_send, w_recv, z, other)
            if name == "cz":
                for sign in (1, -1)[: 1 if ab[0] == 8 else 2]:
                    ref = zero_half(plane(sign * ab[0]))
                    send(ref, ref, w_send, w_recv, z, other)
            elif name in CORE:
                for at in CORE[name]:
                    src = ctx_in if name == "cO" else blk(*at)
                    send(src, blk(*at), ctx_send, c_recv, z, other)
            elif name == "z":
                n, part = ab
                sem = pk_recv.at[(n - 1) * 3 + part]
                signs = (1, -1) if n < 8 else (1,) if part < 2 else (-1,)
                if act == "W":
                    wait_bytes(pk.at[pl.ds(0, len(signs)), pl.ds(0, ZSUB), :], sem)
                    continue
                hop = 2 if n <= FAST and n % 2 == 0 else 1
                if n == hop and part > 0 and not waited:
                    waited = True
                    wait_bytes(zero_half(z), w_recv)
                for sign in signs:
                    ref = pk_sub(plane(sign * (hop - n)), part)
                    send(ref, ref, pk_send, sem, plane(sign * hop), t)
            elif act == "S":
                for at, half, to in SENDS[name]:
                    dst = blk(*at, half)
                    send(ctx_in if at == (0, 0) else dst, dst, ctx_send, g_recv.at[NAMES.index(name)], z, dev(*to))
            else:
                wait_bytes(ctx.at[pl.ds(0, BLOCKS[name] * BLK), :], g_recv.at[NAMES.index(name)])
        if c == 0:
            wait_bytes(pk.at[pl.ds(0, NZ - 1), pl.ds(0, PK), :], w_recv)

    @pl.when(is_zero)
    def _():
        gather(0)

    @pl.when(is_one)
    def _():
        gather(1)

    for c in loads[5:]:
        c.wait()
    gainb[...] = jnp.transpose(jnp.broadcast_to(grow[...], (128, ROWS)))
    biasb[...] = jnp.transpose(jnp.broadcast_to(brow[...], (128, ROWS)))
    for j in range(NZ):
        c = 192 * j
        stk[0:192, c : c + 128] = pk[j, pl.ds(half_at, 192), :]
        stk[0:96, c + 128 : c + 192] = pk[j, pl.ds(half_at + 192, 96), 0:64]
        stk[96:192, c + 128 : c + 192] = pk[j, pl.ds(half_at + 192, 96), 64:128]
    wait_bytes(ctx.at[pl.ds(0, 16 * BLK), :], c_recv)
    for c in loads[1:5]:
        c.wait()

    for n in range(2):
        cols = slice(n * 512, (n + 1) * 512)
        both = jnp.dot(stk[...], ctx[:, cols], preferred_element_type=F32)
        xv[:, cols] = both[0:192]
        tau[:, cols] = both[192:384]

    def sums(i, carry):
        k = lax.rem(2 * x + 4 + i, 8)
        lanes = pl.ds(pl.multiple_of(k * 128, 128), 128)
        tot = jnp.zeros((16, 128), F32)
        for r in range(12):
            rows = pl.ds(r * 16, 16)
            xx = xv[rows, lanes] + res[rows, lanes].astype(F32)
            xv[rows, lanes] = xx
            tot = tot + xx
        mean = jnp.sum(tot, axis=0, keepdims=True) / ROWS
        accs = [jnp.zeros((16, 128), F32) for _ in range(11)]
        for r in range(12):
            rows = pl.ds(r * 16, 16)
            yy = xv[rows, lanes] - mean
            tt = tau[rows, lanes]
            g = gainb[rows, :]
            w = g * g
            h = g * (biasb[rows, :] - tgt[rows, lanes].astype(F32))
            wy = w * yy
            wt = w * tt
            terms = (yy * yy, wy, wy * yy, h, h * yy, tt, yy * tt, wt, wy * tt, h * tt, w)
            accs = [a + b for a, b in zip(accs, terms)]
        mom[k, 0:1, :] = mean
        for a in range(11):
            mom[k, a + 1 : a + 2, :] = jnp.sum(accs[a], axis=0, keepdims=True)
        mom[k, 12:16, :] = jnp.ones((4, 128), F32)

        @pl.when(t != 4 * k + 1)
        def _():
            send(mom.at[k], mbuf.at[t], mom_send, mom_recv, z, 4 * k + 1)

        return carry

    lax.fori_loop(0, 8, sums, 0)
    mine = lax.div(t, 4)
    is_owner = lax.rem(t, 4) == 1

    @pl.when(is_owner)
    def _():
        mbuf[t] = mom[mine]
        wait_bytes(mbuf.at[pl.ds(0, NT - 1)], mom_recv)
        s0 = mbuf[0]
        for i in range(1, NT):
            s0 = s0 + mbuf[i]
        mean = s0[0:1] / NT
        s1 = jnp.zeros((16, 128), F32)
        s2 = jnp.zeros((16, 128), F32)
        for i in range(NT):
            m = mbuf[i]
            dm = (m[0:1] - mean) * m
            s1 = s1 + dm
            s2 = s2 + (m[0:1] - mean) * dm

        def row(a, i):
            return a[i : i + 1]

        s_w = row(s0, 11)
        s_h = row(s0, 4)
        s_t = row(s0, 6)
        s_wt = row(s0, 8)
        s_ht = row(s0, 10)
        s_zz = row(s0, 1) + ROWS * row(s2, 12)
        s_wz = row(s0, 2) + row(s1, 11)
        s_wzz = row(s0, 3) + 2 * row(s1, 2) + row(s2, 11)
        s_hz = row(s0, 5) + row(s1, 4)
        s_zt = row(s0, 7) + row(s1, 6)
        s_wzt = row(s0, 9) + row(s1, 8)
        sc = 1.0 / jnp.sqrt(s_zz / D + 1e-05)
        s_wn = sc * s_wz
        s_wnn = sc * sc * s_wzz
        s_hn = sc * s_hz
        g_mean = (s_wn + s_h) / D
        g_proj = (s_wnn + s_hn) / D
        t_mean = s_t / D
        t_proj = sc * s_zt / D
        c_mean = sc * (s_wt - t_mean * s_w - t_proj * s_wn) / D
        c_proj = sc * (2 * (sc * s_wzt - t_mean * s_wn - t_proj * s_wnn) + s_ht - t_mean * s_h - t_proj * s_hn) / D
        for i, v in enumerate((mean, sc, g_mean, g_proj, t_mean, t_proj, c_mean, c_proj)):
            cbuf[mine, i : i + 1, :] = v

        steps = sorted(((dx, dy) for dx in range(4) for dy in range(4)), key=lambda d: -min(d[0], 4 - d[0]) - min(d[1], 4 - d[1]))
        for dx, dy in steps:
            chip = lax.rem(x + dx, 4) * 8 + lax.rem(y + dy, 4) * 2
            for c in (0, 1):
                if (dx, dy, c) != (0, 0, 1):
                    send(cbuf.at[mine], cbuf.at[mine], cf_send, cf_recv.at[mine], z, chip + c)

    def finish(i, carry):
        k = lax.rem(2 * x + 6 + i, 8)

        @pl.when(t != 4 * k + 1)
        def _():
            wait_bytes(cbuf.at[k], cf_recv.at[k])

        lanes = pl.ds(pl.multiple_of(k * 128, 128), 128)
        mean, sc, g_mean, g_proj, t_mean, t_proj, c_mean, c_proj = [cbuf[k, a : a + 1, :] for a in range(8)]
        lead = -sc * t_proj
        for r in range(12):
            rows = pl.ds(r * 16, 16)
            n = (xv[rows, lanes] - mean) * sc
            g = gainb[rows, :]
            w = g * g
            gn = g * (g * n + biasb[rows, :] - tgt[rows, lanes].astype(F32))
            grad = sc * (gn - g_mean - n * g_proj)
            rg[rows, lanes] = grad
            u = sc * (tau[rows, lanes] - t_mean - n * t_proj)
            cv = lead * grad + sc * (w * u - c_mean - u * g_proj - n * c_proj)
            curv[rows, :] = cv
            if r >= 8:
                curv[pl.ds(r * 16 + 64, 16), :] = cv
        curvt[pl.ds(pl.multiple_of(k * 128, 128), 128), :] = jnp.transpose(curv[...]).astype(BF16)
        return carry

    lax.fori_loop(0, 8, finish, 0)
    rg_copy = pltpu.make_async_copy(rg, rg_out, load_sem.at[5])
    rg_copy.start()

    lane = lax.broadcasted_iota(jnp.int32, (96, 128), 1)

    def pack(full, to, slot):
        to[slot, 0:192, :] = full[:, 0:128]
        to[slot, 192:288, :] = jnp.where(lane < 64, full[0:96, 128:256], full[96:192, 128:256])

    def product(i, to, slot):
        rows = pl.ds(pl.multiple_of(wanted(i) * 192, 64), 192)
        pack(jnp.dot(ctx[rows, :], curvt[...], preferred_element_type=F32), to, slot)

    def products():
        for b in range(4):
            full = jnp.dot(ctx[768 * b : 768 * (b + 1), :], curvt[...], preferred_element_type=F32)
            for i in range(4):
                pack(full[192 * i : 192 * (i + 1)], prod, 4 * b + i)

    def wanted(i):
        return plane(8 + (1 - 2 * lax.rem(i, 2)) * lax.div(i + 1, 2))

    def finish_hess(both):
        pair = stk[192:384, pl.ds(pl.multiple_of(lax.div(z, 2) * 384, 128), 384)].astype(F32)
        pc = jnp.where(lax.rem(z, 2) == 0, pair[:, 0:192], pair[:, 192:384]) * (1.0 / TOKENS)
        at = jnp.transpose(both[0:192])
        bt = jnp.transpose(both[192:288])
        hess_ref[0:128, :] = pc[0:128] * at
        hess_ref[128:192, 0:96] = pc[128:192, 0:96] * bt[0:64]
        hess_ref[128:192, 96:192] = pc[128:192, 96:192] * bt[64:128]

    def rs_sub(w, n, s):
        return rs.at[(w * 9 + n) * 4 + s]

    def rs_sem(w, n, s):
        return rs_recv.at[(w * 8 + n - 1) * 4 + s]

    def rs_take(w, n, s):
        wait_bytes(rs_sub(w, n, s), rs_sem(w, n, s))

    def decode(w, n, s):
        at = (w * 9 + n) * 4 + s
        near = rs[at, 0:RSUB, :].astype(F32)
        low = rs[at, RSUB:RMSG, :].astype(F32)
        one = jnp.round(low * (1 / 21))
        two = low - 21 * one
        steps = jnp.concatenate([one, two[0:64]], axis=0)
        return near + near * (steps * LOW)

    def last_of(first):
        parts = []
        for s in (first, first + 1):
            for w in range(2):
                rs_take(w, 8, s)
            parts.append(decode(0, 8, s) + decode(1, 8, s))
        finish_hess(prod[z] + jnp.concatenate(parts, axis=0))

    @pl.when(is_zero)
    def _():
        for group, (lo, hi) in enumerate(GROUPS):

            def hand(i, carry, group=group):
                product(i, prod, wanted(i))
                send(prod.at[wanted(i)], prod0.at[i], prod_send, prod_recv.at[group], z, other)
                return carry

            lax.fori_loop(lo, hi, hand, 0)
        product(NZ - 1, prod, z)
        last_of(2)
        wait_bytes(prod.at[pl.ds(0, NZ - 1)], prod_send)

    @pl.when(is_one)
    def _():
        def rs_pass(w, n, s):
            to = other if n == 7 and s > 1 else t
            send(rs_sub(w, n, s), rs_sub(w, n + 1, s), rs_send, rs_sem(w, n + 1, s), plane(1 - 2 * w), to)

        def own(i, s):
            lo = s % 2 * RSUB
            if s > 1:
                return prod0[i, lo : lo + RSUB, :]
            return early[i // 2, lo : lo + RSUB, :] if i in (0, 2) else prod[wanted(i), lo : lo + RSUB, :]

        def code(w, n, s, v):
            at = (w * 9 + n) * 4 + s
            high = v.astype(BF16)
            near = high.astype(F32)
            rest = jnp.where(jnp.abs(near) > 1e-30, (v - near) * pl.reciprocal(near, approx=True), 0.0)
            steps = jnp.round(rest * (1 / LOW))
            rs[at, 0:RSUB, :] = high
            rs[at, RSUB : RSUB + 64, :] = (21 * steps[0:64] + steps[80:RSUB]).astype(BF16)
            rs[at, RSUB + 64 : RMSG, :] = (21 * steps[64:80]).astype(BF16)

        def put(w, n, i, s, add):
            v = own(i, s)
            if add:
                rs_take(w, n, s)
                v = v + decode(w, n, s)
            code(w, n, s, v)
            rs_pass(w, n, s)

        def theirs(group):
            lo, hi = GROUPS[group]
            wait_bytes(prod0.at[pl.ds(lo, hi - lo)], prod_recv.at[group])

        product(0, early, 0)
        for s in (0, 1):
            put(0, 0, 0, s, False)
        theirs(0)
        for s in (2, 3):
            put(1, 0, 0, s, False)
        product(2, early, 1)
        for s in (0, 1):
            put(1, 1, 2, s, False)
        theirs(1)
        for s in (2, 3):
            put(0, 1, 1, s, False)
        products()
        theirs(2)
        for s in (0, 1):
            put(0, 1, 1, s, True)
            put(1, 1, 2, s + 2, True)
        for n in range(2, 8):
            if n < 5:
                theirs(n + 1)
            for s in (2, 3, 0, 1):
                put(0, n, 2 * n - 1, s, True)
                put(1, n, 2 * n, s ^ 2, True)
        last_of(0)
        wait_bytes(rs.at[pl.ds(0, 60)], rs_send)
        wait_bytes(pk.at[pl.ds(0, 15)], pk_send)
        wait_bytes(pk.at[pl.ds(0, 15), pl.ds(0, PK), :], w_send)

    rg_copy.wait()
    wait_bytes(ctx.at[pl.ds(0, 31 * BLK), :], ctx_send)

    @pl.when(is_zero)
    def _():
        wait_bytes(pk.at[0, pl.ds(0, PK), :], w_send)

    @pl.when(is_owner)
    def _():
        wait_bytes(mom.at[pl.ds(0, 7)], mom_send)
        wait_bytes(prod.at[0, pl.ds(0, 8 * (NT - 1)), :], cf_send)

    @pl.when(jnp.logical_not(is_owner))
    def _():
        wait_bytes(mom, mom_send)


def shards(context, residual, out_weight, norm_gain, norm_bias, target, probe):
    hbm = pl.BlockSpec(memory_space=pltpu.HBM)
    anywhere = pl.BlockSpec(memory_space=pl.ANY)
    vmem = pl.BlockSpec(memory_space=pltpu.VMEM)
    dma = pltpu.SemaphoreType.DMA
    arrays = (context, residual, out_weight, norm_gain.reshape(1, ROWS), norm_bias.reshape(1, ROWS), target, probe)
    arrays = [pltpu.with_memory_space_constraint(a, pltpu.HBM) for a in arrays]
    return pl.pallas_call(
        kernel,
        out_shape=(
            jax.ShapeDtypeStruct((ROWS, 192), F32),
            jax.ShapeDtypeStruct((ROWS, TOK), F32),
        ),
        in_specs=[hbm] * 7,
        out_specs=(vmem, anywhere),
        scratch_shapes=[
            pltpu.VMEM((NT * BLK, TOK), BF16),
            pltpu.VMEM((2 * ROWS, 3072), BF16),
            pltpu.VMEM((NZ, 2 * PK, 128), BF16),
            pltpu.VMEM((192, 192), BF16),
            pltpu.VMEM((ROWS, TOK), BF16),
            pltpu.VMEM((ROWS, TOK), BF16),
            pltpu.VMEM((ROWS, TOK), F32),
            pltpu.VMEM((ROWS, TOK), F32),
            pltpu.VMEM((1, ROWS), F32),
            pltpu.VMEM((1, ROWS), F32),
            pltpu.VMEM((ROWS, 128), F32),
            pltpu.VMEM((ROWS, 128), F32),
            pltpu.VMEM((8, 16, 128), F32),
            pltpu.VMEM((NT, 16, 128), F32),
            pltpu.VMEM((8, 8, 128), F32),
            pltpu.VMEM((256, 128), F32),
            pltpu.VMEM((TOK, 256), BF16),
            pltpu.VMEM((ROWS, TOK), F32),
            pltpu.VMEM((18 * 4, RMSG, 128), BF16),
            pltpu.VMEM((2, PK, 128), F32),
            pltpu.VMEM((NZ, PK, 128), F32),
            pltpu.VMEM((NZ, PK, 128), F32),
            dma((8,)),
            dma,
            dma((9,)),
            dma,
            dma,
            dma((24,)),
            dma,
            dma,
            dma,
            dma,
            dma,
            dma((8,)),
            dma,
            dma((64,)),
            dma,
            dma((len(GROUPS),)),
        ],
        compiler_params=pltpu.CompilerParams(
            collective_id=0, has_side_effects=True, vmem_limit_bytes=48 * 1024 * 1024
        ),
    )(*arrays)


def solution(mesh):
    return jax.shard_map(
        shards,
        mesh=mesh,
        in_specs=(
            P("tensor", "dp"),
            P("tensor", "dp"),
            P("tensor", "dp"),
            P("tensor"),
            P("tensor"),
            P("tensor", "dp"),
            P("tensor", None),
        ),
        out_specs=(P("tensor", "dp"), P("tensor", "dp")),
        check_vma=False,
    )
```

```python
import jax
import jax.numpy as jnp
from jax import lax
from jax.experimental import pallas as pl
from jax.experimental.pallas import tpu as pltpu
from jax.sharding import PartitionSpec as P

MESH = pl.DeviceIdType.MESH
F32 = jnp.float32
BF16 = jnp.bfloat16

D = 6144
ROWS = 192
TOK = 1024
BLK = 96
NZ = 16
NT = 32
PK = 288
ZSUB = 192
RSUB = 144
RMSG = 224
LOW = 2.0**-8 / 10
GROUPS = ((0, 1), (1, 2), (2, 3), (3, 5), (5, 7), (7, 15))
FAST = 2 * 3
TOKENS = 16384

PLAN = (
    (
        ("S", "cO"), ("S", "P"), ("S", "Q0"), ("W", "P"), ("S", "Q1"), ("S", "P2"), ("W", "P2"), ("S", "QA"),
        ("S", "cP2"), ("S", "cP"), ("W", "Q0"), ("S", "QQ0"), ("S", "QB"), ("W", "Q1"), ("S", "QQ1"), ("S", "cQ0"),
        ("W", "QA"), ("S", "QQ2"), ("S", "cQ1"), ("W", "QB"), ("W", "QQ0"), ("S", "cQ2"), ("W", "QQ1"), ("S", "cQQ1"),
        ("S", "cQQ0"), ("W", "QQ2"), ("S", "cQQ2"),
    ),
    (
        ("S", "P"), ("S", "z", 2, 0), ("S", "z", 2, 1), ("S", "cO"), ("S", "z", 2, 2), ("S", "z", 1, 2),
        ("W", "z", 2, 0), ("S", "Q0"), ("S", "z", 4, 0), ("W", "z", 1, 2), ("S", "z", 1, 1), ("S", "z", 1, 0),
        ("W", "P"), ("S", "P2"), ("W", "z", 2, 1), ("S", "z", 4, 1), ("W", "z", 2, 2), ("S", "Q1"), ("W", "z", 4, 0),
        ("S", "z", 4, 2), ("W", "z", 1, 0), ("S", "z", 3, 2), ("S", "z", 6, 0), ("W", "z", 1, 1), ("W", "z", 4, 1),
        ("S", "cz", 2), ("S", "z", 6, 1), ("W", "Q0"), ("S", "cP"), ("W", "P2"), ("S", "z", 3, 1), ("S", "QA"),
        ("W", "z", 4, 2), ("S", "z", 6, 2), ("S", "cP2"), ("S", "QB"), ("W", "z", 6, 0), ("S", "QQ0"),
        ("S", "z", 7, 0), ("S", "cz", 4), ("W", "Q1"), ("S", "z", 5, 1), ("S", "cQ1"), ("W", "z", 6, 1),
        ("S", "z", 7, 1), ("S", "QQ1"), ("S", "cQ0"), ("S", "z", 5, 0), ("W", "z", 3, 1), ("W", "z", 6, 2),
        ("S", "z", 7, 2), ("S", "cz", 1), ("W", "QB"), ("W", "QA"), ("W", "z", 5, 1), ("S", "z", 3, 0),
        ("S", "z", 5, 2), ("S", "cQ2"), ("W", "z", 3, 2), ("W", "z", 7, 1), ("S", "cz", 6), ("S", "QQ2"),
        ("S", "cz", 3), ("W", "z", 7, 0), ("S", "z", 8, 1), ("W", "z", 5, 0), ("W", "QQ0"), ("W", "z", 7, 2),
        ("S", "z", 8, 2), ("S", "cQQ0"), ("S", "cz", 7), ("W", "QQ1"), ("S", "z", 8, 0), ("S", "cQQ1"),
        ("W", "z", 5, 2), ("S", "cz", 5), ("W", "z", 8, 1), ("W", "QQ2"), ("S", "cQQ2"), ("W", "z", 8, 2),
        ("S", "cz", 8), ("W", "z", 3, 0), ("W", "z", 8, 0),
    ),
)
SENDS = {
    "P": (((0, 0), None, (1, 0)), ((0, 0), None, (-1, 0))),
    "P2": (((-1, 0), 0, (1, 0)), ((1, 0), 1, (-1, 0))),
    "Q0": (((0, 0), None, (0, 1)), ((0, 0), None, (0, -1))),
    "Q1": tuple(((a, 0), None, (0, b)) for a in (-1, 1) for b in (1, -1)),
    "QA": (((2, 0), 0, (0, 1)), ((2, 0), 1, (0, -1))),
    "QB": (((2, 0), 0, (0, -1)), ((2, 0), 1, (0, 1))),
    "QQ0": (((0, -1), 0, (0, 1)), ((0, 1), 1, (0, -1))),
    "QQ1": tuple(((a, -b), (1 - b) // 2, (0, b)) for a in (-1, 1) for b in (1, -1)),
    "QQ2": (((2, -1), 0, (0, 1)), ((2, 1), 1, (0, -1))),
}
NAMES = tuple(SENDS)
BLOCKS = {"P": 2, "P2": 1, "Q0": 2, "Q1": 4, "QA": 1, "QB": 1, "QQ0": 1, "QQ1": 2, "QQ2": 1}
CORE = {
    "cO": ((0, 0),),
    "cP": ((-1, 0), (1, 0)),
    "cP2": ((2, 0),),
    "cQ0": ((0, -1), (0, 1)),
    "cQ1": ((-1, -1), (-1, 1), (1, -1), (1, 1)),
    "cQ2": ((2, -1), (2, 1)),
    "cQQ0": ((0, 2),),
    "cQQ1": ((-1, 2), (1, 2)),
    "cQQ2": ((2, 2),),
}


def kernel(
    ctx_in, res_in, w_in, gain_in, bias_in, tgt_in, probe_in,
    hess_ref, rg_out,
    ctx, stk, pk, wloc, res, tgt, xv, tau, grow, brow, gainb, biasb, mom, mbuf, cbuf, curv, curvt, rg, rs, early, prod, prod0,
    load_sem, ctx_send, g_recv, c_recv, pk_send, pk_recv, w_send, w_recv,
    mom_send, mom_recv, cf_send, cf_recv, rs_send, rs_recv, prod_send, prod_recv,
):
    z = lax.axis_index("dp")
    t = lax.axis_index("tensor")
    core = lax.rem(t, 2)
    x = lax.div(t, 8)
    y = lax.rem(lax.div(t, 2), 4)
    other = t + 1 - 2 * core
    is_one = core == 1
    is_zero = core == 0

    def plane(n):
        return lax.rem(z + n + NZ, NZ)


    def wait_bytes(ref, sem):
        pltpu.make_async_copy(ref, ref, sem).wait()

    def send(src, dst, ssem, rsem, zz, tt):
        pltpu.make_async_remote_copy(
            src_ref=src, dst_ref=dst, send_sem=ssem, recv_sem=rsem, device_id=(zz, tt), device_id_type=MESH
        ).start()

    weight_load = pltpu.make_async_copy(w_in, wloc, load_sem.at[0])
    weight_load.start()
    barrier = pltpu.get_barrier_semaphore()
    for n in (1, -1, 2, -2):
        pl.semaphore_signal(barrier, inc=1, device_id=(plane(n), t), device_id_type=MESH)
    for n in (1, -1):
        pl.semaphore_signal(barrier, inc=1, device_id=(plane(n), other), device_id_type=MESH)

    def greet(i, carry):
        pl.semaphore_signal(barrier, inc=1, device_id=(z, lax.rem(t + i, NT)), device_id_type=MESH)
        return carry

    lax.fori_loop(1, NT, greet, 0)

    own_rows = pl.ds(pl.multiple_of(t * BLK, 32), BLK)
    own = ctx.at[own_rows, :]
    loads = [
        weight_load,
        pltpu.make_async_copy(probe_in, stk.at[pl.ds(ROWS, ROWS), :], load_sem.at[1]),
        pltpu.make_async_copy(ctx_in, own, load_sem.at[2]),
        pltpu.make_async_copy(res_in, res, load_sem.at[3]),
        pltpu.make_async_copy(tgt_in, tgt, load_sem.at[4]),
        pltpu.make_async_copy(gain_in, grow, load_sem.at[6]),
        pltpu.make_async_copy(bias_in, brow, load_sem.at[7]),
    ]
    for c in loads[1:]:
        c.start()
    pl.semaphore_wait(barrier, NT + 5)

    half_at = pl.multiple_of((1 - core) * PK, 32)

    def pack_weight():
        loads[0].wait()
        pk[z, pl.ds(half_at, 192), :] = wloc[:, 0:128]
        pk[z, pl.ds(half_at + 192, 96), 0:64] = wloc[0:96, 128:192]
        pk[z, pl.ds(half_at + 192, 96), 64:128] = wloc[96:192, 128:192]

    def zero_half(j):
        return pk.at[j, pl.ds(PK, PK), :]

    def pk_sub(j, s):
        return pk.at[j, pl.ds(s * ZSUB, ZSUB), :]

    def gather(c):
        p, q = (y, x) if c else (x, y)
        sp, sq = (2, 8) if c else (8, 2)

        def dev(dp, dq):
            return lax.rem(p + dp + 4, 4) * sp + lax.rem(q + dq + 4, 4) * sq + c

        def rows_of(dp, dq):
            return pl.ds(pl.multiple_of(dev(dp, dq) * BLK, 32), BLK)

        def blk(dp, dq, half=None):
            rows = rows_of(dp, dq)
            return ctx.at[rows, :] if half is None else ctx.at[rows, pl.ds(half * 512, 512)]

        packed = waited = False
        for act, name, *ab in PLAN[c]:
            if not packed and (act == "W" or name == "z"):
                packed = True
                pack_weight()
                if c == 0:
                    send(zero_half(z), zero_half(z), w_send, w_recv, z, other)
            if name == "cz":
                for sign in (1, -1)[: 1 if ab[0] == 8 else 2]:
                    ref = zero_half(plane(sign * ab[0]))
                    send(ref, ref, w_send, w_recv, z, other)
            elif name in CORE:
                for at in CORE[name]:
                    src = ctx_in if name == "cO" else blk(*at)
                    send(src, blk(*at), ctx_send, c_recv, z, other)
            elif name == "z":
                n, part = ab
                sem = pk_recv.at[(n - 1) * 3 + part]
                signs = (1, -1) if n < 8 else (1,) if part < 2 else (-1,)
                if act == "W":
                    wait_bytes(pk.at[pl.ds(0, len(signs)), pl.ds(0, ZSUB), :], sem)
                    continue
                hop = 2 if n <= FAST and n % 2 == 0 else 1
                if n == hop and part > 0 and not waited:
                    waited = True
                    wait_bytes(zero_half(z), w_recv)
                for sign in signs:
                    ref = pk_sub(plane(sign * (hop - n)), part)
                    send(ref, ref, pk_send, sem, plane(sign * hop), t)
            elif act == "S":
                for at, half, to in SENDS[name]:
                    dst = blk(*at, half)
                    send(ctx_in if at == (0, 0) else dst, dst, ctx_send, g_recv.at[NAMES.index(name)], z, dev(*to))
            else:
                wait_bytes(ctx.at[pl.ds(0, BLOCKS[name] * BLK), :], g_recv.at[NAMES.index(name)])
        if c == 0:
            wait_bytes(pk.at[pl.ds(0, NZ - 1), pl.ds(0, PK), :], w_recv)

    @pl.when(is_zero)
    def _():
        gather(0)

    @pl.when(is_one)
    def _():
        gather(1)

    for c in loads[5:]:
        c.wait()
    gainb[...] = jnp.transpose(jnp.broadcast_to(grow[...], (128, ROWS)))
    biasb[...] = jnp.transpose(jnp.broadcast_to(brow[...], (128, ROWS)))
    for j in range(NZ):
        c = 192 * j
        stk[0:192, c : c + 128] = pk[j, pl.ds(half_at, 192), :]
        stk[0:96, c + 128 : c + 192] = pk[j, pl.ds(half_at + 192, 96), 0:64]
        stk[96:192, c + 128 : c + 192] = pk[j, pl.ds(half_at + 192, 96), 64:128]
    wait_bytes(ctx.at[pl.ds(0, 16 * BLK), :], c_recv)
    for c in loads[1:5]:
        c.wait()

    for n in range(2):
        cols = slice(n * 512, (n + 1) * 512)
        both = jnp.dot(stk[...], ctx[:, cols], preferred_element_type=F32)
        xv[:, cols] = both[0:192]
        tau[:, cols] = both[192:384]

    def sums(i, carry):
        k = lax.rem(2 * x + 4 + i, 8)
        lanes = pl.ds(pl.multiple_of(k * 128, 128), 128)
        tot = jnp.zeros((16, 128), F32)
        for r in range(12):
            rows = pl.ds(r * 16, 16)
            xx = xv[rows, lanes] + res[rows, lanes].astype(F32)
            xv[rows, lanes] = xx
            tot = tot + xx
        mean = jnp.sum(tot, axis=0, keepdims=True) / ROWS
        accs = [jnp.zeros((16, 128), F32) for _ in range(11)]
        for r in range(12):
            rows = pl.ds(r * 16, 16)
            yy = xv[rows, lanes] - mean
            tt = tau[rows, lanes]
            g = gainb[rows, :]
            w = g * g
            h = g * (biasb[rows, :] - tgt[rows, lanes].astype(F32))
            wy = w * yy
            wt = w * tt
            terms = (yy * yy, wy, wy * yy, h, h * yy, tt, yy * tt, wt, wy * tt, h * tt, w)
            accs = [a + b for a, b in zip(accs, terms)]
        mom[k, 0:1, :] = mean
        for a in range(11):
            mom[k, a + 1 : a + 2, :] = jnp.sum(accs[a], axis=0, keepdims=True)
        mom[k, 12:16, :] = jnp.ones((4, 128), F32)

        @pl.when(t != 4 * k + 1)
        def _():
            send(mom.at[k], mbuf.at[t], mom_send, mom_recv, z, 4 * k + 1)

        return carry

    lax.fori_loop(0, 8, sums, 0)
    mine = lax.div(t, 4)
    is_owner = lax.rem(t, 4) == 1

    @pl.when(is_owner)
    def _():
        mbuf[t] = mom[mine]
        wait_bytes(mbuf.at[pl.ds(0, NT - 1)], mom_recv)
        s0 = mbuf[0]
        for i in range(1, NT):
            s0 = s0 + mbuf[i]
        mean = s0[0:1] / NT
        s1 = jnp.zeros((16, 128), F32)
        s2 = jnp.zeros((16, 128), F32)
        for i in range(NT):
            m = mbuf[i]
            dm = (m[0:1] - mean) * m
            s1 = s1 + dm
            s2 = s2 + (m[0:1] - mean) * dm

        def row(a, i):
            return a[i : i + 1]

        s_w = row(s0, 11)
        s_h = row(s0, 4)
        s_t = row(s0, 6)
        s_wt = row(s0, 8)
        s_ht = row(s0, 10)
        s_zz = row(s0, 1) + ROWS * row(s2, 12)
        s_wz = row(s0, 2) + row(s1, 11)
        s_wzz = row(s0, 3) + 2 * row(s1, 2) + row(s2, 11)
        s_hz = row(s0, 5) + row(s1, 4)
        s_zt = row(s0, 7) + row(s1, 6)
        s_wzt = row(s0, 9) + row(s1, 8)
        sc = 1.0 / jnp.sqrt(s_zz / D + 1e-05)
        s_wn = sc * s_wz
        s_wnn = sc * sc * s_wzz
        s_hn = sc * s_hz
        g_mean = (s_wn + s_h) / D
        g_proj = (s_wnn + s_hn) / D
        t_mean = s_t / D
        t_proj = sc * s_zt / D
        c_mean = sc * (s_wt - t_mean * s_w - t_proj * s_wn) / D
        c_proj = sc * (2 * (sc * s_wzt - t_mean * s_wn - t_proj * s_wnn) + s_ht - t_mean * s_h - t_proj * s_hn) / D
        for i, v in enumerate((mean, sc, g_mean, g_proj, t_mean, t_proj, c_mean, c_proj)):
            cbuf[mine, i : i + 1, :] = v

        steps = sorted(((dx, dy) for dx in range(4) for dy in range(4)), key=lambda d: -min(d[0], 4 - d[0]) - min(d[1], 4 - d[1]))
        for dx, dy in steps:
            chip = lax.rem(x + dx, 4) * 8 + lax.rem(y + dy, 4) * 2
            for c in (0, 1):
                if (dx, dy, c) != (0, 0, 1):
                    send(cbuf.at[mine], cbuf.at[mine], cf_send, cf_recv.at[mine], z, chip + c)

    def finish(i, carry):
        k = lax.rem(2 * x + 6 + i, 8)

        @pl.when(t != 4 * k + 1)
        def _():
            wait_bytes(cbuf.at[k], cf_recv.at[k])

        lanes = pl.ds(pl.multiple_of(k * 128, 128), 128)
        mean, sc, g_mean, g_proj, t_mean, t_proj, c_mean, c_proj = [cbuf[k, a : a + 1, :] for a in range(8)]
        lead = -sc * t_proj
        for r in range(12):
            rows = pl.ds(r * 16, 16)
            n = (xv[rows, lanes] - mean) * sc
            g = gainb[rows, :]
            w = g * g
            gn = g * (g * n + biasb[rows, :] - tgt[rows, lanes].astype(F32))
            grad = sc * (gn - g_mean - n * g_proj)
            rg[rows, lanes] = grad
            u = sc * (tau[rows, lanes] - t_mean - n * t_proj)
            cv = lead * grad + sc * (w * u - c_mean - u * g_proj - n * c_proj)
            curv[rows, :] = cv
            if r >= 8:
                curv[pl.ds(r * 16 + 64, 16), :] = cv
        curvt[pl.ds(pl.multiple_of(k * 128, 128), 128), :] = jnp.transpose(curv[...]).astype(BF16)
        return carry

    lax.fori_loop(0, 8, finish, 0)
    rg_copy = pltpu.make_async_copy(rg, rg_out, load_sem.at[5])

    lane = lax.broadcasted_iota(jnp.int32, (96, 128), 1)

    def pack(full, to, slot):
        to[slot, 0:192, :] = full[:, 0:128]
        to[slot, 192:288, :] = jnp.where(lane < 64, full[0:96, 128:256], full[96:192, 128:256])

    def product(i, to, slot):
        rows = pl.ds(pl.multiple_of(wanted(i) * 192, 64), 192)
        pack(jnp.dot(ctx[rows, :], curvt[...], preferred_element_type=F32), to, slot)

    def products():
        for b in range(4):
            full = jnp.dot(ctx[768 * b : 768 * (b + 1), :], curvt[...], preferred_element_type=F32)
            for i in range(4):
                pack(full[192 * i : 192 * (i + 1)], prod, 4 * b + i)

    def wanted(i):
        return plane(8 + (1 - 2 * lax.rem(i, 2)) * lax.div(i + 1, 2))

    def finish_hess(both):
        pair = stk[192:384, pl.ds(pl.multiple_of(lax.div(z, 2) * 384, 128), 384)].astype(F32)
        pc = jnp.where(lax.rem(z, 2) == 0, pair[:, 0:192], pair[:, 192:384]) * (1.0 / TOKENS)
        at = jnp.transpose(both[0:192])
        bt = jnp.transpose(both[192:288])
        hess_ref[0:128, :] = pc[0:128] * at
        hess_ref[128:192, 0:96] = pc[128:192, 0:96] * bt[0:64]
        hess_ref[128:192, 96:192] = pc[128:192, 96:192] * bt[64:128]

    def rs_sub(w, n, s):
        return rs.at[(w * 9 + n) * 4 + s]

    def rs_sem(w, n, s):
        return rs_recv.at[(w * 8 + n - 1) * 4 + s]

    def rs_take(w, n, s):
        wait_bytes(rs_sub(w, n, s), rs_sem(w, n, s))

    def decode(w, n, s):
        at = (w * 9 + n) * 4 + s
        near = rs[at, 0:RSUB, :].astype(F32)
        low = rs[at, RSUB:RMSG, :].astype(F32)
        one = jnp.round(low * (1 / 21))
        two = low - 21 * one
        steps = jnp.concatenate([one, two[0:64]], axis=0)
        return near + near * (steps * LOW)

    def last_of(first):
        parts = []
        for s in (first, first + 1):
            for w in range(2):
                rs_take(w, 8, s)
            parts.append(decode(0, 8, s) + decode(1, 8, s))
        finish_hess(prod[z] + jnp.concatenate(parts, axis=0))

    @pl.when(is_zero)
    def _():
        for group, (lo, hi) in enumerate(GROUPS):

            def hand(i, carry, group=group):
                product(i, prod, wanted(i))
                send(prod.at[wanted(i)], prod0.at[i], prod_send, prod_recv.at[group], z, other)
                return carry

            lax.fori_loop(lo, hi, hand, 0)
        product(NZ - 1, prod, z)
        rg_copy.start()
        last_of(2)
        wait_bytes(prod.at[pl.ds(0, NZ - 1)], prod_send)

    @pl.when(is_one)
    def _():
        def rs_pass(w, n, s):
            to = other if n == 7 and s > 1 else t
            send(rs_sub(w, n, s), rs_sub(w, n + 1, s), rs_send, rs_sem(w, n + 1, s), plane(1 - 2 * w), to)

        def own(i, s):
            lo = s % 2 * RSUB
            if s > 1:
                return prod0[i, lo : lo + RSUB, :]
            return early[i // 2, lo : lo + RSUB, :] if i in (0, 2) else prod[wanted(i), lo : lo + RSUB, :]

        def code(w, n, s, v):
            at = (w * 9 + n) * 4 + s
            high = v.astype(BF16)
            near = high.astype(F32)
            rest = jnp.where(jnp.abs(near) > 1e-30, (v - near) * pl.reciprocal(near, approx=True), 0.0)
            steps = jnp.round(rest * (1 / LOW))
            rs[at, 0:RSUB, :] = high
            rs[at, RSUB : RSUB + 64, :] = (21 * steps[0:64] + steps[80:RSUB]).astype(BF16)
            rs[at, RSUB + 64 : RMSG, :] = (21 * steps[64:80]).astype(BF16)

        def put(w, n, i, s, add):
            v = own(i, s)
            if add:
                rs_take(w, n, s)
                v = v + decode(w, n, s)
            code(w, n, s, v)
            rs_pass(w, n, s)

        def theirs(group):
            lo, hi = GROUPS[group]
            wait_bytes(prod0.at[pl.ds(lo, hi - lo)], prod_recv.at[group])

        product(0, early, 0)
        for s in (0, 1):
            put(0, 0, 0, s, False)
        theirs(0)
        for s in (2, 3):
            put(1, 0, 0, s, False)
        product(2, early, 1)
        for s in (0, 1):
            put(1, 1, 2, s, False)
        theirs(1)
        for s in (2, 3):
            put(0, 1, 1, s, False)
        rg_copy.start()
        products()
        theirs(2)
        for s in (0, 1):
            put(0, 1, 1, s, True)
            put(1, 1, 2, s + 2, True)
        for n in range(2, 8):
            if n < 5:
                theirs(n + 1)
            for s in (2, 3, 0, 1):
                put(0, n, 2 * n - 1, s, True)
                put(1, n, 2 * n, s ^ 2, True)
        last_of(0)
        wait_bytes(rs.at[pl.ds(0, 60)], rs_send)
        wait_bytes(pk.at[pl.ds(0, 15)], pk_send)
        wait_bytes(pk.at[pl.ds(0, 15), pl.ds(0, PK), :], w_send)

    rg_copy.wait()
    wait_bytes(ctx.at[pl.ds(0, 31 * BLK), :], ctx_send)

    @pl.when(is_zero)
    def _():
        wait_bytes(pk.at[0, pl.ds(0, PK), :], w_send)

    @pl.when(is_owner)
    def _():
        wait_bytes(mom.at[pl.ds(0, 7)], mom_send)
        wait_bytes(prod.at[0, pl.ds(0, 8 * (NT - 1)), :], cf_send)

    @pl.when(jnp.logical_not(is_owner))
    def _():
        wait_bytes(mom, mom_send)


def shards(context, residual, out_weight, norm_gain, norm_bias, target, probe):
    hbm = pl.BlockSpec(memory_space=pltpu.HBM)
    anywhere = pl.BlockSpec(memory_space=pl.ANY)
    vmem = pl.BlockSpec(memory_space=pltpu.VMEM)
    dma = pltpu.SemaphoreType.DMA
    arrays = (context, residual, out_weight, norm_gain.reshape(1, ROWS), norm_bias.reshape(1, ROWS), target, probe)
    arrays = [pltpu.with_memory_space_constraint(a, pltpu.HBM) for a in arrays]
    return pl.pallas_call(
        kernel,
        out_shape=(
            jax.ShapeDtypeStruct((ROWS, 192), F32),
            jax.ShapeDtypeStruct((ROWS, TOK), F32),
        ),
        in_specs=[hbm] * 7,
        out_specs=(vmem, anywhere),
        scratch_shapes=[
            pltpu.VMEM((NT * BLK, TOK), BF16),
            pltpu.VMEM((2 * ROWS, 3072), BF16),
            pltpu.VMEM((NZ, 2 * PK, 128), BF16),
            pltpu.VMEM((192, 192), BF16),
            pltpu.VMEM((ROWS, TOK), BF16),
            pltpu.VMEM((ROWS, TOK), BF16),
            pltpu.VMEM((ROWS, TOK), F32),
            pltpu.VMEM((ROWS, TOK), F32),
            pltpu.VMEM((1, ROWS), F32),
            pltpu.VMEM((1, ROWS), F32),
            pltpu.VMEM((ROWS, 128), F32),
            pltpu.VMEM((ROWS, 128), F32),
            pltpu.VMEM((8, 16, 128), F32),
            pltpu.VMEM((NT, 16, 128), F32),
            pltpu.VMEM((8, 8, 128), F32),
            pltpu.VMEM((256, 128), F32),
            pltpu.VMEM((TOK, 256), BF16),
            pltpu.VMEM((ROWS, TOK), F32),
            pltpu.VMEM((18 * 4, RMSG, 128), BF16),
            pltpu.VMEM((2, PK, 128), F32),
            pltpu.VMEM((NZ, PK, 128), F32),
            pltpu.VMEM((NZ, PK, 128), F32),
            dma((8,)),
            dma,
            dma((9,)),
            dma,
            dma,
            dma((24,)),
            dma,
            dma,
            dma,
            dma,
            dma,
            dma((8,)),
            dma,
            dma((64,)),
            dma,
            dma((len(GROUPS),)),
        ],
        compiler_params=pltpu.CompilerParams(
            collective_id=0, has_side_effects=True, vmem_limit_bytes=48 * 1024 * 1024
        ),
    )(*arrays)


def solution(mesh):
    return jax.shard_map(
        shards,
        mesh=mesh,
        in_specs=(
            P("tensor", "dp"),
            P("tensor", "dp"),
            P("tensor", "dp"),
            P("tensor"),
            P("tensor"),
            P("tensor", "dp"),
            P("tensor", None),
        ),
        out_specs=(P("tensor", "dp"), P("tensor", "dp")),
        check_vma=False,
    )
```
